128 devices in a mesh: dp: 8 (over y, core), group: 16 (over x, z).
Axes of the slice: x: 4, y: 4, z: 4, core: 2. Of those that a mesh axis runs over, the one named last changes fastest.
Arguments:
- tile_maps: bfloat16 [1024, 16, 16, 384], P(('dp', 'group')), may hold values from -45 to 45
- positions: int32 [2, 1024], P(None, ('dp', 'group')), may hold values from 0 to 511
- counts: int32 [8], P('dp'), may hold values from 1 to 128, as said below
- routing: int32 [8, 16, 8], P(None, 'group'), may hold values from -1 to 31, as said below
- depth_kernel: float32 [49, 384], replicated, may hold values from -0.875 to 0.875
- depth_bias: float32 [384], replicated, may hold values from -3 to 3
- norm_gain: float32 [384], replicated, may hold values from 0.25 to 1.75
- norm_shift: float32 [384], replicated, may hold values from -2 to 2
- expand_weight: bfloat16 [384, 1536], replicated, may hold values from -0.3125 to 0.3125
- expand_bias: float32 [1536], replicated, may hold values from -1.15 to -0.75
- reduce_weight: bfloat16 [1536, 384], replicated, may hold values from -0.15625 to 0.15625
- reduce_bias: float32 [384], replicated, may hold values from -2 to 2
- layer_scale: float32 [384], replicated, may hold values from 0.3 to 1.5
- head_weight: bfloat16 [384, 768], replicated, may hold values from -0.3125 to 0.3125
- slide_taps: float32 [7, 768], replicated, may hold values from -2.5 to 2.5
- slide_weight: bfloat16 [768, 768], replicated, may hold values from -0.21875 to 0.21875
- slide_bias: float32 [768], replicated, may hold values from -2 to 2
- cotangent: float32 [8, 768], P('dp'), may hold values from -180 to 180
Outputs:
- tile_out: bfloat16 [512, 16, 16, 384], P(('dp', 'group'))
- slide_feature: float32 [8, 768], P('dp')
- grad_expand: float32 [589824], P(('dp', 'group'))
- grad_reduce: float32 [589824], P(('dp', 'group'))
- grad_depth: float32 [18816], P(('dp', 'group'))
The draws below stay inside these ranges and needn't reach their ends.
Inputs may be any that keep to these rules, and one draw needn't show every extreme that they name: counts[d] is the number of tiles of slide d. At each group index the present tiles of all slides number at most 32, at group index 0 exactly that. routing[d, g, s] is -1 where the slot holds no tile, else e * 4 + p: the tile is processed at slot p of the device with dp index e and group index g. Each processing slot receives at most one tile; at group index 0 every one receives a tile. A device sends at most 1 tiles to each dp index, and some device sends exactly 1 to each.
All inputs are finite; a program needn't handle non-finite values.
Results may differ from the reference program's by a relative error of at most 0.013.
Values may be sent and summed in bfloat16 or wider, within the bound.
A program may use at most 128 MiB of HBM per device.

```python
import math
import jax
import jax.numpy as jnp
from jax import lax

C = 384
HID = 1536
E = 768
KS = 7
TH = 16
KERNEL_TAPS = 7
TILE_DILATION = 3
PROC = 4
SLIDES = 8
GSIZE = 16
SLOTS = 8
SEQ = 128
TILES = 1024
PTILES = 512


def slide_plan(key):
    base_key = jax.random.fold_in(key, 7001)
    busy = jax.random.randint(jax.random.fold_in(base_key, 1), (), 0, SLIDES)
    slide_ids = jnp.arange(SLIDES, dtype=jnp.int32)
    others = slide_ids != busy
    weights = jnp.where(others, jax.random.randint(jax.random.fold_in(base_key, 2), (SLIDES,), 2, 5), 0)
    avail = SLIDES * PROC - SLOTS - (SLIDES - 1)
    shares = avail * weights // jnp.sum(weights)
    leftover = avail - jnp.sum(shares)
    other_rank = jnp.cumsum(others.astype(jnp.int32)) - 1
    extra = jnp.where(others & (other_rank < leftover), 1, 0)
    per_device = jnp.where(others, 1 + shares + extra, SLOTS)
    tails = jax.random.randint(jax.random.fold_in(base_key, 3), (SLIDES,), 1, GSIZE + 1)
    tails = jnp.where(others, tails, GSIZE)
    return (GSIZE * (per_device - 1) + tails).astype(jnp.int32)


def draw_counts(key, part):
    return slide_plan(key)


def draw_routing(key, part):
    slide_counts = slide_plan(key)
    base_key = jax.random.fold_in(key, 7002)
    slot_ids = jnp.arange(SLOTS, dtype=jnp.int32)
    member_ids = jnp.arange(GSIZE, dtype=jnp.int32)
    present = slot_ids[None, None, :] * GSIZE + member_ids[None, :, None] < slide_counts[:, None, None]
    column = jnp.transpose(present, (1, 0, 2)).reshape(GSIZE, SLIDES * SLOTS).astype(jnp.int32)
    placed = jnp.cumsum(column, axis=1) - column
    dest_keys = jax.random.split(jax.random.fold_in(base_key, 1), GSIZE)
    dest_perm = jax.vmap(lambda one_key: jax.random.permutation(one_key, SLIDES))(dest_keys).astype(jnp.int32)
    slot_key_list = jax.random.split(jax.random.fold_in(base_key, 2), GSIZE * SLIDES)
    slot_perm = jax.vmap(lambda one_key: jax.random.permutation(one_key, PROC))(slot_key_list).astype(jnp.int32).reshape(GSIZE, SLIDES * PROC)
    receiver = jnp.take_along_axis(dest_perm, placed % SLIDES, axis=1)
    depth_rank = jnp.minimum(placed // SLIDES, PROC - 1)
    processor_slot = jnp.take_along_axis(slot_perm, receiver * PROC + depth_rank, axis=1)
    routed = jnp.where(column > 0, receiver * PROC + processor_slot, -1)
    return jnp.transpose(routed.reshape(GSIZE, SLIDES, SLOTS), (1, 0, 2)).astype(jnp.int32)


def draw_tile_maps(key, part):
    base_key = jax.random.fold_in(key, 7003)
    shape_all = (TILES, TH, TH, C)
    channel_scale = jnp.exp(jax.random.uniform(jax.random.fold_in(base_key, 2), (C,), jnp.float32, jnp.log(0.3), jnp.log(3.0)))
    cell_scale = jnp.exp(jax.random.uniform(jax.random.fold_in(base_key, 3), (TILES, TH, TH, 1), jnp.float32, jnp.log(0.4), jnp.log(2.5)))
    values = jnp.clip(jax.random.normal(jax.random.fold_in(base_key, 1), shape_all, jnp.float32), -6.0, 6.0)
    return (values * channel_scale * cell_scale).astype(jnp.bfloat16)


def place_ends(values, rng, low, largest):
    longest = values.shape.index(max(values.shape))
    spots = []
    for shift in (0, 1):
        where = [jax.random.randint(jax.random.fold_in(rng, axis), (), 0, length) for axis, length in enumerate(values.shape)]
        where[longest] = (where[longest] + shift) % values.shape[longest]
        spots.append(tuple(where))
    return values.at[spots[0]].set(low).at[spots[1]].set(largest)


def steps_of(key, shape, cuts, least, top_value):
    level = 1.0
    for dim, shards_of in cuts:
        draws = jax.random.uniform(jax.random.fold_in(jax.random.fold_in(key, 6), dim), (shards_of,), jnp.float32, least / len(cuts), top_value / len(cuts))
        level = level * jnp.repeat(jnp.exp(draws), shape[dim] // shards_of).reshape((-1,) + (1,) * (len(shape) - 1 - dim))
    return level


def bell_draw(rng, shape, spread, reach, cuts=(), kind=jnp.bfloat16):
    array = jax.random.normal(rng, shape, jnp.float32) * spread
    if len(cuts) > 0:
        array = steps_of(rng, shape, cuts, -0.22, 0.18) * array
    return jnp.clip(array, min=-reach, max=reach).astype(kind)


def setup_inputs(seed: int = 0) -> dict:
    seeds = jax.random.split(jax.random.key(seed), 19)
    return {
        "tile_maps": draw_tile_maps(jax.random.fold_in(seeds[18], 71), 0),
        "positions": place_ends(jax.random.randint(seeds[1], (2, TILES), 0, 512), jax.random.fold_in(seeds[1], 1), 0, 511).astype(jnp.int32),
        "counts": draw_counts(jax.random.fold_in(seeds[18], 71), 0),
        "routing": draw_routing(jax.random.fold_in(seeds[18], 71), 0),
        "depth_kernel": bell_draw(seeds[4], (KS * KS, C), (KS * KS) ** -0.5, 0.875, (), jnp.float32),
        "depth_bias": bell_draw(seeds[5], (C,), 0.5, 3.0, (), jnp.float32),
        "norm_gain": jnp.clip(1.0 + 0.15 * jax.random.normal(seeds[6], (C,), jnp.float32), 0.25, 1.75),
        "norm_shift": bell_draw(seeds[7], (C,), 0.3, 2.0, (), jnp.float32),
        "expand_weight": bell_draw(seeds[8], (C, HID), C ** -0.5, 0.3125),
        "expand_bias": jnp.clip(jax.random.uniform(seeds[9], (HID,), jnp.float32, -1.15, -0.75), -1.15, -0.75),
        "reduce_weight": bell_draw(seeds[10], (HID, C), HID ** -0.5, 0.15625),
        "reduce_bias": bell_draw(seeds[11], (C,), 0.3, 2.0, (), jnp.float32),
        "layer_scale": jnp.clip(jnp.exp(jax.random.uniform(seeds[12], (C,), jnp.float32, math.log(0.3), math.log(1.5))), 0.3, 1.5),
        "head_weight": bell_draw(seeds[13], (C, E), C ** -0.5, 0.3125),
        "slide_taps": bell_draw(seeds[14], (KERNEL_TAPS, E), 0.4, 2.5, (), jnp.float32),
        "slide_weight": bell_draw(seeds[15], (E, E), E ** -0.5, 0.21875),
        "slide_bias": bell_draw(seeds[16], (E,), 0.3, 2.0, (), jnp.float32),
        "cotangent": bell_draw(seeds[17], (SLIDES, E), 30.0, 180.0, ((0, 8),), jnp.float32),
    }


EPSILON = 1e-06
HALF_ROOT = 0.7071067811865476
INV_ROOT_TAU = 0.3989422804014327

def gelu_exact(values):
    return 0.5 * values * (1.0 + jax.scipy.special.erf(values * HALF_ROOT))

def gelu_slope(values):
    return 0.5 * (1.0 + jax.scipy.special.erf(values * HALF_ROOT)) + values * INV_ROOT_TAU * jnp.exp(-0.5 * values * values)

def contract_rows(left_side, right_side):
    return lax.dot_general(left_side, right_side, (((0,), (0,)), ((), ())), preferred_element_type=jnp.float32)

def contract_cols(left_side, right_side):
    return lax.dot_general(left_side, right_side, (((1,), (1,)), ((), ())), preferred_element_type=jnp.float32)

def padded_tiles(work_tiles):
    border_width = KS // 2
    return jnp.pad(work_tiles, ((0, 0), (border_width, border_width), (border_width, border_width), (0, 0)))

def block_forward(work_tiles, depth_kernel, depth_bias, norm_gain, norm_shift, expand_weight, expand_bias, reduce_weight, reduce_bias, layer_scale, head_weight):
    tile_count = work_tiles.shape[0]
    tile_side = work_tiles.shape[1]
    channels = work_tiles.shape[3]
    pixels = tile_side * tile_side
    padded = padded_tiles(work_tiles)
    running = jnp.zeros(work_tiles.shape, jnp.float32) + depth_bias
    for tap_row in range(KS):
        for tap_col in range(KS):
            running = running + depth_kernel[tap_row * KS + tap_col] * padded[:, tap_row:tap_row + tile_side, tap_col:tap_col + tile_side]
    depth_out = running.reshape(tile_count * pixels, channels)
    chan_mean = lax.optimization_barrier(jnp.mean(depth_out, axis=1, keepdims=True))
    centred = depth_out - chan_mean
    inv_std = lax.rsqrt(lax.optimization_barrier(jnp.mean(centred * centred, axis=1, keepdims=True)) + EPSILON)
    unit_norm = centred * inv_std
    normed = (unit_norm * norm_gain + norm_shift).astype(jnp.bfloat16)
    pre_act = jnp.dot(normed, expand_weight, preferred_element_type=jnp.float32) + expand_bias
    hidden = gelu_exact(pre_act).astype(jnp.bfloat16)
    mlp_out = jnp.dot(hidden, reduce_weight, preferred_element_type=jnp.float32) + reduce_bias
    section_rows = (work_tiles.reshape(tile_count * pixels, channels) + layer_scale * mlp_out).astype(jnp.bfloat16)
    head_pre = jnp.dot(section_rows, head_weight, preferred_element_type=jnp.float32)
    tile_embed = lax.optimization_barrier(jnp.mean(gelu_exact(head_pre).reshape(tile_count, pixels, -1), axis=1)).astype(jnp.bfloat16)
    return (section_rows.reshape(work_tiles.shape), tile_embed, (unit_norm, inv_std, normed, pre_act, hidden, head_pre))

def block_backward(work_tiles, saved_acts, embed_grad, norm_gain, expand_weight, reduce_weight, layer_scale, head_weight):
    unit_norm, inv_std, normed, pre_act, hidden, head_pre = saved_acts
    tile_count = work_tiles.shape[0]
    tile_side = work_tiles.shape[1]
    channels = work_tiles.shape[3]
    pixels = tile_side * tile_side
    slope_head = gelu_slope(head_pre).reshape(tile_count, pixels, -1)
    grad_head = (embed_grad.astype(jnp.float32)[:, None, :] / float(pixels) * slope_head).astype(jnp.bfloat16)
    grad_head = grad_head.reshape(tile_count * pixels, -1)
    grad_block = contract_cols(grad_head, head_weight)
    grad_mlp = (layer_scale * grad_block).astype(jnp.bfloat16)
    reduce_grad = contract_rows(hidden, grad_mlp)
    grad_hidden = contract_cols(grad_mlp, reduce_weight)
    grad_pre = (grad_hidden * gelu_slope(pre_act)).astype(jnp.bfloat16)
    expand_grad = contract_rows(normed, grad_pre)
    grad_norm = contract_cols(grad_pre, expand_weight)
    scaled_grad = grad_norm * norm_gain
    grad_depthwise = inv_std * (scaled_grad - lax.optimization_barrier(jnp.mean(scaled_grad, axis=1, keepdims=True)) - unit_norm * lax.optimization_barrier(jnp.mean(scaled_grad * unit_norm, axis=1, keepdims=True)))
    grad_depthwise = grad_depthwise.reshape(tile_count, tile_side, tile_side, channels)
    padded = padded_tiles(work_tiles)
    tap_grads = []
    for tap_row in range(KS):
        for tap_col in range(KS):
            tap_grads.append(lax.optimization_barrier(jnp.sum(grad_depthwise * padded[:, tap_row:tap_row + tile_side, tap_col:tap_col + tile_side], axis=(0, 1, 2))))
    return (expand_grad, reduce_grad, jnp.stack(tap_grads))

def position_code(positions):
    half_width = E // 2
    channel_ids = jnp.arange(half_width, dtype=jnp.int32)
    frequency = jnp.exp((2 * (channel_ids // 2)).astype(jnp.float32) * (-math.log(10000.0) / half_width))
    pieces = []
    for coord_axis in range(2):
        angles = positions[coord_axis].astype(jnp.float32)[:, None] * frequency[None, :]
        pieces.append(jnp.where(channel_ids % 2 == 0, jnp.sin(angles), jnp.cos(angles)))
    return jnp.concatenate(pieces, axis=1)

def dilate(seq_float, slide_taps, travel_direction):
    length = seq_float.shape[0]
    border_width = KERNEL_TAPS // 2 * TILE_DILATION
    padded = jnp.pad(seq_float, ((border_width, border_width), (0, 0)))
    running = jnp.zeros(seq_float.shape, jnp.float32)
    for shift_amount in range(KERNEL_TAPS):
        leading_row = border_width + travel_direction * (shift_amount - KERNEL_TAPS // 2) * TILE_DILATION
        running = running + slide_taps[shift_amount] * padded[leading_row:leading_row + length]
    return running

def slide_pass(sequence, seq_present, slide_count, slide_cot, slide_taps, slide_weight, slide_bias):
    seq_float = sequence.astype(jnp.float32)
    mixed = (seq_float + dilate(seq_float, slide_taps, 1)).astype(jnp.bfloat16)
    agg_pre = jnp.dot(mixed, slide_weight, preferred_element_type=jnp.float32) + slide_bias
    weight = seq_present.astype(jnp.float32) / slide_count.astype(jnp.float32)
    feature = lax.optimization_barrier(jnp.sum(gelu_exact(agg_pre) * weight[:, None], axis=0))
    grad_agg = (slide_cot[None, :] * weight[:, None] * gelu_slope(agg_pre)).astype(jnp.bfloat16)
    grad_mixed = contract_cols(grad_agg, slide_weight)
    seq_grad = ((grad_mixed + dilate(grad_mixed, slide_taps, -1)) * seq_present.astype(jnp.float32)[:, None]).astype(jnp.bfloat16)
    return (feature, seq_grad)

def reference(tile_maps, positions, counts, routing, depth_kernel, depth_bias, norm_gain, norm_shift, expand_weight, expand_bias, reduce_weight, reduce_bias, layer_scale, head_weight, slide_taps, slide_weight, slide_bias, cotangent):
    params = (depth_kernel, depth_bias, norm_gain, norm_shift, expand_weight, expand_bias, reduce_weight, reduce_bias, layer_scale, head_weight)
    tile_ids = jnp.arange(TILES, dtype=jnp.int32)
    group_of = tile_ids // SLOTS % GSIZE
    slide_of = tile_ids // (GSIZE * SLOTS)
    seq_index = tile_ids % SLOTS * GSIZE + group_of
    present = seq_index < counts[slide_of]
    route_flat = routing.reshape(-1)
    routed = route_flat >= 0
    target = jnp.where(routed, (route_flat // PROC * GSIZE + group_of) * PROC + route_flat % PROC, PTILES).astype(jnp.int32)
    source = jnp.full((PTILES,), -1, jnp.int32).at[target].set(tile_ids, mode='drop')
    filled = source >= 0
    safe_index = jnp.maximum(source, 0).astype(jnp.int32)

    def forward_one(tile_index):
        work_tiles = lax.dynamic_index_in_dim(tile_maps, tile_index, 0, keepdims=True)
        section_out, tile_embed, _ = block_forward(work_tiles, *params)
        return (section_out[0], tile_embed[0])
    tile_outs, tile_embeds = lax.map(forward_one, safe_index)
    tile_out = jnp.where(filled[:, None, None, None], tile_outs, jnp.zeros((), jnp.bfloat16))
    owner_index = jnp.where(filled, source, TILES).astype(jnp.int32)
    owner_emb = jnp.zeros((TILES, E), jnp.bfloat16).at[owner_index].set(tile_embeds, mode='drop')
    pos_code = position_code(positions)
    slide_rows = jnp.where(present[:, None], (owner_emb.astype(jnp.float32) + pos_code).astype(jnp.bfloat16), jnp.zeros((), jnp.bfloat16))
    seq_all = slide_rows.reshape(SLIDES, GSIZE, SLOTS, E).transpose(0, 2, 1, 3).reshape(SLIDES, SEQ, E)
    present_all = present.reshape(SLIDES, GSIZE, SLOTS).transpose(0, 2, 1).reshape(SLIDES, SEQ)

    def slide_one(slide_item):
        return slide_pass(slide_item[0], slide_item[1], slide_item[2], slide_item[3], slide_taps, slide_weight, slide_bias)
    features, seq_grads = lax.map(slide_one, (seq_all, present_all, counts, cotangent))
    row_grads = seq_grads.reshape(SLIDES, SLOTS, GSIZE, E).transpose(0, 2, 1, 3).reshape(TILES, E)
    embed_grads = jnp.where(filled[:, None], row_grads[safe_index], jnp.zeros((), jnp.bfloat16))

    def back_one(totals, scan_item):
        tile_index, grad_row = scan_item
        work_tiles = lax.dynamic_index_in_dim(tile_maps, tile_index, 0, keepdims=True)
        _, _, saved_acts = block_forward(work_tiles, *params)
        expand_grad, reduce_grad, depth_grad = block_backward(work_tiles, saved_acts, grad_row[None, :], norm_gain, expand_weight, reduce_weight, layer_scale, head_weight)
        return ((totals[0] + expand_grad, totals[1] + reduce_grad, totals[2] + depth_grad), None)
    zero_grads = (jnp.zeros((C, HID), jnp.float32), jnp.zeros((HID, C), jnp.float32), jnp.zeros((KS * KS, C), jnp.float32))
    sums, _ = lax.scan(back_one, zero_grads, (safe_index, embed_grads))
    return (tile_out, features, sums[0].reshape(-1), sums[1].reshape(-1), sums[2].reshape(-1))
```

```python
import math

import jax
import jax.numpy as jnp
from jax import lax
from jax.experimental import pallas as pl
from jax.experimental.pallas import tpu as pltpu
from jax.sharding import PartitionSpec as P

E = 768
KS = 7
KERNEL_TAPS = 7
TILE_DILATION = 3
PROC = 4


EPSILON = 1e-06
HALF_ROOT = 0.7071067811865476
INV_ROOT_TAU = 0.3989422804014327


def gelu_exact(values):
    return 0.5 * values * (1.0 + jax.scipy.special.erf(values * HALF_ROOT))


def gelu_slope(values):
    return 0.5 * (
        1.0 + jax.scipy.special.erf(values * HALF_ROOT)
    ) + values * INV_ROOT_TAU * jnp.exp(-0.5 * values * values)


def contract_rows(left_side, right_side):
    return lax.dot_general(
        left_side, right_side, (((0,), (0,)), ((), ())), preferred_element_type=jnp.float32
    )


def contract_cols(left_side, right_side):
    return lax.dot_general(
        left_side, right_side, (((1,), (1,)), ((), ())), preferred_element_type=jnp.float32
    )


def padded_tiles(work_tiles):
    border_width = KS // 2
    return jnp.pad(
        work_tiles, ((0, 0), (border_width, border_width), (border_width, border_width), (0, 0))
    )


def block_forward(
    work_tiles,
    depth_kernel,
    depth_bias,
    norm_gain,
    norm_shift,
    expand_weight,
    expand_bias,
    reduce_weight,
    reduce_bias,
    layer_scale,
    head_weight,
):
    tile_count = work_tiles.shape[0]
    tile_side = work_tiles.shape[1]
    channels = work_tiles.shape[3]
    pixels = tile_side * tile_side
    padded = padded_tiles(work_tiles)
    running = jnp.zeros(work_tiles.shape, jnp.float32) + depth_bias
    for tap_row in range(KS):
        for tap_col in range(KS):
            running = (
                running
                + depth_kernel[tap_row * KS + tap_col]
                * padded[:, tap_row : tap_row + tile_side, tap_col : tap_col + tile_side]
            )
    depth_out = running.reshape(tile_count * pixels, channels)
    chan_mean = jnp.mean(depth_out, axis=1, keepdims=True)
    centred = depth_out - chan_mean
    inv_std = lax.rsqrt(jnp.mean(centred * centred, axis=1, keepdims=True) + EPSILON)
    unit_norm = centred * inv_std
    normed = (unit_norm * norm_gain + norm_shift).astype(jnp.bfloat16)
    pre_act = jnp.dot(normed, expand_weight, preferred_element_type=jnp.float32) + expand_bias
    hidden = gelu_exact(pre_act).astype(jnp.bfloat16)
    mlp_out = jnp.dot(hidden, reduce_weight, preferred_element_type=jnp.float32) + reduce_bias
    section_rows = (
        work_tiles.reshape(tile_count * pixels, channels) + layer_scale * mlp_out
    ).astype(jnp.bfloat16)
    head_pre = jnp.dot(section_rows, head_weight, preferred_element_type=jnp.float32)
    tile_embed = jnp.mean(gelu_exact(head_pre).reshape(tile_count, pixels, -1), axis=1).astype(
        jnp.bfloat16
    )
    return (
        section_rows.reshape(work_tiles.shape),
        tile_embed,
        (unit_norm, inv_std, normed, pre_act, hidden, head_pre),
    )


def block_backward(
    work_tiles,
    saved_acts,
    embed_grad,
    norm_gain,
    expand_weight,
    reduce_weight,
    layer_scale,
    head_weight,
):
    unit_norm, inv_std, normed, pre_act, hidden, head_pre = saved_acts
    tile_count = work_tiles.shape[0]
    tile_side = work_tiles.shape[1]
    channels = work_tiles.shape[3]
    pixels = tile_side * tile_side
    slope_head = gelu_slope(head_pre).reshape(tile_count, pixels, -1)
    grad_head = (embed_grad.astype(jnp.float32)[:, None, :] / float(pixels) * slope_head).astype(
        jnp.bfloat16
    )
    grad_head = grad_head.reshape(tile_count * pixels, -1)
    grad_block = contract_cols(grad_head, head_weight)
    grad_mlp = (layer_scale * grad_block).astype(jnp.bfloat16)
    reduce_grad = contract_rows(hidden, grad_mlp)
    grad_hidden = contract_cols(grad_mlp, reduce_weight)
    grad_pre = (grad_hidden * gelu_slope(pre_act)).astype(jnp.bfloat16)
    expand_grad = contract_rows(normed, grad_pre)
    grad_norm = contract_cols(grad_pre, expand_weight)
    scaled_grad = grad_norm * norm_gain
    grad_depthwise = inv_std * (
        scaled_grad
        - jnp.mean(scaled_grad, axis=1, keepdims=True)
        - unit_norm * jnp.mean(scaled_grad * unit_norm, axis=1, keepdims=True)
    )
    grad_depthwise = grad_depthwise.reshape(tile_count, tile_side, tile_side, channels)
    padded = padded_tiles(work_tiles)
    tap_grads = []
    for tap_row in range(KS):
        for tap_col in range(KS):
            tap_grads.append(
                jnp.sum(
                    grad_depthwise
                    * padded[:, tap_row : tap_row + tile_side, tap_col : tap_col + tile_side],
                    axis=(0, 1, 2),
                )
            )
    return (expand_grad, reduce_grad, jnp.stack(tap_grads))


def position_code(positions):
    half_width = E // 2
    channel_ids = jnp.arange(half_width, dtype=jnp.int32)
    frequency = jnp.exp(
        (2 * (channel_ids // 2)).astype(jnp.float32) * (-math.log(10000.0) / half_width)
    )
    pieces = []
    for coord_axis in range(2):
        angles = positions[coord_axis].astype(jnp.float32)[:, None] * frequency[None, :]
        pieces.append(jnp.where(channel_ids % 2 == 0, jnp.sin(angles), jnp.cos(angles)))
    return jnp.concatenate(pieces, axis=1)


MESH = pl.DeviceIdType.MESH
PARTS = (32, 32, 16)
ORDERS = ("yxz", "xzy", "zyx")
ROWS = sum(PARTS)

def torus_place():
    dp, group = lax.axis_index("dp"), lax.axis_index("group")
    return {"y": lax.div(dp, 2), "c": lax.rem(dp, 2), "x": lax.div(group, 4), "z": lax.rem(group, 4)}

def torus_device(place, **moved):
    at = {**place, **moved}
    return (at["y"] * 2 + at["c"], at["x"] * 4 + at["z"])

def reduce_scatter_kernel(grads, out, core_in, s1, s2, s3, r1, r2, r3, core_send, core_recv, send, recv):
    place = torus_place()
    partner = torus_device(place, c=1 - place["c"])
    barrier = pltpu.get_barrier_semaphore()
    pl.semaphore_signal(barrier, inc=1, device_id=partner, device_id_type=MESH)
    for axis in "yxz":
        for k in (1, 2, 3):
            pl.semaphore_signal(barrier, inc=1, device_id=torus_device(place, **{axis: lax.rem(place[axis] + k, 4)}), device_id_type=MESH)
    pl.semaphore_wait(barrier, 10)

    core_copies = []
    for y in range(4):
        cp = pltpu.make_async_remote_copy(src_ref=grads.at[y, 1 - place["c"]], dst_ref=core_in.at[y], send_sem=core_send.at[y], recv_sem=core_recv.at[y], device_id=partner, device_id_type=MESH)
        cp.start()
        core_copies.append(cp)

    def start(stage, part, source, landing):
        axis = ORDERS[part][stage]
        made = []
        for k in (2, 1, 3):
            to = lax.rem(place[axis] + k, 4)
            cp = pltpu.make_async_remote_copy(src_ref=source.at[to], dst_ref=landing.at[k - 1], send_sem=send.at[stage * 9 + part * 3 + k - 1], recv_sem=recv.at[stage * 9 + part * 3 + k - 1], device_id=torus_device(place, **{axis: to}), device_id_type=MESH)
            cp.start()
            made.append(cp)
        return made

    f32 = jnp.float32
    for y in range(4):
        core_copies[y].wait_recv()
        for x in range(4):
            both = grads[y, place["c"], x].astype(f32) + core_in[y, x].astype(f32)
            both = both.astype(jnp.bfloat16)
            s1[0][y, x] = both[:, 0:32]
            s1[1][x, :, y] = both[:, 32:64]
            for z in range(4):
                s1[2][z, y, x] = both[z, 64:80]
    flying = [start(0, part, s1[part], r1[part]) for part in range(3)]
    flying2 = []
    for part in range(3):
        for cp in flying[part]:
            cp.wait_recv()
        mine = place[ORDERS[part][0]]
        for a in range(4):
            total = s1[part][mine, a].astype(f32)
            for k in range(3):
                total = total + r1[part][k, a].astype(f32)
            s2[part][a] = total.astype(jnp.bfloat16)
        flying2.append(start(1, part, s2[part], r2[part]))
    flying3 = []
    for part in range(3):
        for cp in flying2[part]:
            cp.wait_recv()
        mine = place[ORDERS[part][1]]
        total = s2[part][mine].astype(f32)
        for k in range(3):
            total = total + r2[part][k].astype(f32)
        s3[part][...] = total.astype(jnp.bfloat16)
        flying3.append(start(2, part, s3[part], r3[part]))
    base = 0
    for part in range(3):
        for cp in flying3[part]:
            cp.wait_recv()
        total = s3[part][place[ORDERS[part][2]]].astype(f32)
        for k in range(3):
            total = total + r3[part][k].astype(f32)
        out[base:base + PARTS[part]] = total
        base += PARTS[part]
    for cp in core_copies:
        cp.wait_send()
    for copies in flying + flying2 + flying3:
        for cp in copies:
            cp.wait_send()

def reduce_scatter(grads):
    bf16 = jnp.bfloat16
    buf = lambda *lead: [pltpu.VMEM(lead + (rows, 128), bf16) for rows in PARTS]
    return pl.pallas_call(
        reduce_scatter_kernel,
        out_shape=jax.ShapeDtypeStruct((ROWS, 128), jnp.float32),
        in_specs=[pl.BlockSpec(memory_space=pltpu.VMEM)],
        out_specs=pl.BlockSpec(memory_space=pltpu.VMEM),
        scratch_shapes=[
            pltpu.VMEM((4, 4, 4, ROWS, 128), bf16),
            buf(4, 4, 4), buf(4, 4), buf(4), buf(3, 4, 4), buf(3, 4), buf(3),
            pltpu.SemaphoreType.DMA((4,)), pltpu.SemaphoreType.DMA((4,)),
            pltpu.SemaphoreType.DMA((27,)), pltpu.SemaphoreType.DMA((27,)),
        ],
        compiler_params=pltpu.CompilerParams(collective_id=1, has_side_effects=True, vmem_limit_bytes=32 * 2**20),
        name="grad_reduce_scatter",
    )(grads)


def slide_kernel(count, embeds, own_pick, take_pick, pos_code, taps, weight, bias, cot, feature, embed_grad,
                 emb_all, rows_mine, rows_all, wide, grad_wide, grad_mine, grad_all,
                 send1, recv1, send2, recv2, send3, recv3):
    f32, bf16 = jnp.float32, jnp.bfloat16
    dp, group = lax.axis_index("dp"), lax.axis_index("group")
    barrier = pltpu.get_barrier_semaphore()
    dp_peers = [lax.rem(dp + k, 8) for k in range(1, 8)]
    group_peers = [lax.rem(group + k, 16) for k in range(1, 16)]
    for to in dp_peers:
        pl.semaphore_signal(barrier, inc=1, device_id=(to, group), device_id_type=MESH)
    for to in group_peers:
        pl.semaphore_signal(barrier, inc=1, device_id=(dp, to), device_id_type=MESH)
    pl.semaphore_wait(barrier, 22)

    def over_dp(source, landing, send, recv):
        copies = []
        for k, to in enumerate(dp_peers):
            cp = pltpu.make_async_remote_copy(src_ref=source, dst_ref=landing.at[dp], send_sem=send.at[k], recv_sem=recv.at[k], device_id=(to, group), device_id_type=MESH)
            cp.start()
            copies.append(cp)
        landing[dp] = source[...]
        for cp in copies:
            cp.wait()

    over_dp(embeds, emb_all, send1, recv1)
    places = count[0]
    own = jnp.dot(own_pick[...], emb_all[...].reshape(64, 768).astype(bf16), preferred_element_type=f32)
    slot = lax.broadcasted_iota(jnp.int32, (8, 768), 0)
    here = slot * 16 + group < places
    rows_mine[...] = jnp.where(here, (own + pos_code[...]).astype(bf16).astype(f32), 0.0)
    copies = []
    for k, to in enumerate(group_peers):
        cp = pltpu.make_async_remote_copy(src_ref=rows_mine, dst_ref=rows_all.at[group], send_sem=send2.at[k], recv_sem=recv2.at[k], device_id=(dp, to), device_id_type=MESH)
        cp.start()
        copies.append(cp)
    rows_all[group] = rows_mine[...]
    for cp in copies:
        cp.wait()

    def widen(block, target):
        first, last = slot == 0, slot == 7
        target[9:25] = block
        for g in range(9):
            target[g] = jnp.where(first, 0.0, pltpu.roll(block[g + 7], 1, 0))
            target[25 + g] = jnp.where(last, 0.0, pltpu.roll(block[g], 7, 0))

    rows = rows_all[...]
    widen(rows, wide)
    mixed = rows
    for k in range(7):
        mixed = mixed + taps[k] * wide[3 * k:3 * k + 16]
    mixed = mixed.astype(bf16).reshape(128, 768)
    pre = jnp.dot(mixed, weight[...], preferred_element_type=f32) + bias[...]
    row = lax.broadcasted_iota(jnp.int32, (128, 768), 0)
    place = lax.rem(row, 8) * 16 + lax.div(row, 8)
    share = jnp.where(place < places, 1.0, 0.0) / places.astype(f32)
    phi = 0.5 * (1.0 + lax.erf(pre * HALF_ROOT))
    feature[...] = jnp.sum(pre * phi * share, axis=0, keepdims=True)
    slope = phi + pre * INV_ROOT_TAU * jnp.exp(-0.5 * pre * pre)
    grad_agg = (cot[...] * share * slope).astype(bf16)
    grad_mixed = lax.dot_general(grad_agg, weight[...], (((1,), (1,)), ((), ())), preferred_element_type=f32)
    widen(grad_mixed.reshape(16, 8, 768), grad_wide)
    mine = grad_wide[9 + group]
    total = mine
    for k in range(7):
        total = total + taps[k] * grad_wide[group + 18 - 3 * k]
    grad_mine[...] = jnp.where(here, total.astype(bf16).astype(f32), 0.0)
    over_dp(grad_mine, grad_all, send3, recv3)
    embed_grad[...] = jnp.dot(take_pick[...], grad_all[...].reshape(64, 768).astype(bf16), preferred_element_type=f32)

def slide_step(count, embeds, own_pick, take_pick, pos_code, taps, weight, bias, cot):
    f32 = jnp.float32
    vm = pl.BlockSpec(memory_space=pltpu.VMEM)
    sem = lambda n: pltpu.SemaphoreType.DMA((n,))
    return pl.pallas_call(
        slide_kernel,
        out_shape=(jax.ShapeDtypeStruct((1, 768), f32), jax.ShapeDtypeStruct((8, 768), f32)),
        in_specs=[pl.BlockSpec(memory_space=pltpu.SMEM)] + [vm] * 8,
        out_specs=(vm, vm),
        scratch_shapes=[
            pltpu.VMEM((8, 8, 768), f32), pltpu.VMEM((8, 768), f32), pltpu.VMEM((16, 8, 768), f32),
            pltpu.VMEM((34, 8, 768), f32), pltpu.VMEM((34, 8, 768), f32),
            pltpu.VMEM((8, 768), f32), pltpu.VMEM((8, 8, 768), f32),
            sem(7), sem(7), sem(15), sem(15), sem(7), sem(7),
        ],
        compiler_params=pltpu.CompilerParams(collective_id=2, has_side_effects=True, vmem_limit_bytes=32 * 2**20),
        name="slide_step",
    )(count, embeds, own_pick, take_pick, pos_code, taps.reshape(7, 1, 768), weight, bias.reshape(1, 768), cot)


def sender_table(my_list):
    dest_dev = jnp.where(my_list >= 0, my_list // PROC, -1)
    return dest_dev[None, :] == jnp.arange(8, dtype=jnp.int32)[:, None]


def receiver_table(route_rows, my_slide):
    local = route_rows - my_slide * PROC
    hit = (local >= 0) & (local < PROC)
    target = jnp.sum(jnp.where(hit, local, 0), axis=1)
    is_used = jnp.any(hit, axis=1)
    return (target[None, :] == jnp.arange(PROC, dtype=jnp.int32)[:, None]) & is_used[None, :]


def on_device(
    tile_maps,
    positions,
    counts,
    routing,
    depth_kernel,
    depth_bias,
    norm_gain,
    norm_shift,
    expand_weight,
    expand_bias,
    reduce_weight,
    reduce_bias,
    layer_scale,
    head_weight,
    slide_taps,
    slide_weight,
    slide_bias,
    cotangent,
):
    params = (
        depth_kernel,
        depth_bias,
        norm_gain,
        norm_shift,
        expand_weight,
        expand_bias,
        reduce_weight,
        reduce_bias,
        layer_scale,
        head_weight,
    )
    my_slide = lax.axis_index("dp")
    slot_count = tile_maps.shape[0]
    route_rows = routing[:, 0, :]
    my_list = lax.dynamic_index_in_dim(route_rows, my_slide, 0, keepdims=False)
    send_pick = sender_table(my_list).astype(jnp.bfloat16)
    take_bool = receiver_table(route_rows, my_slide)
    take_pick = take_bool.astype(jnp.bfloat16)
    filled = jnp.any(take_bool, axis=1)
    lanes = jnp.arange(64, dtype=jnp.int32)
    place_code = jnp.where(lanes % 8 < PROC, lanes // 8 * PROC + lanes % 8, -2)
    own_pick = (my_list[:, None] == place_code[None, :]).astype(jnp.bfloat16)
    wanted = jnp.where(jnp.arange(8) < PROC, my_slide * PROC + jnp.arange(8), -2)
    grad_pick = (wanted[:, None] == route_rows.reshape(64)[None, :]).astype(jnp.bfloat16)
    pos_code = position_code(positions)
    packed = jnp.dot(
        send_pick, tile_maps.reshape(slot_count, -1), preferred_element_type=jnp.float32
    ).astype(jnp.bfloat16)
    packed = packed.reshape(tile_maps.shape)
    arrived = lax.all_to_all(packed, "dp", split_axis=0, concat_axis=0, tiled=True)
    work_tiles = jnp.dot(
        take_pick, arrived.reshape(slot_count, -1), preferred_element_type=jnp.float32
    ).astype(jnp.bfloat16)
    work_tiles = work_tiles.reshape((PROC,) + tile_maps.shape[1:])
    section_out, tile_embed, saved_acts = block_forward(work_tiles, *params)
    tile_out = jnp.where(filled[:, None, None, None], section_out, jnp.zeros((), jnp.bfloat16))
    embeds = jnp.pad(tile_embed.astype(jnp.float32), ((0, 4), (0, 0)))
    feature, embed_grad = slide_step(
        counts, embeds, own_pick, grad_pick, pos_code, slide_taps, slide_weight, slide_bias, cotangent
    )
    embed_grad = embed_grad[:PROC].astype(jnp.bfloat16)
    source_tiles, _ = lax.optimization_barrier((work_tiles, embed_grad))
    kept_acts = block_forward(source_tiles, *params)[2]
    expand_grad, reduce_grad, depth_grad = block_backward(
        source_tiles,
        kept_acts,
        embed_grad,
        norm_gain,
        expand_weight,
        reduce_weight,
        layer_scale,
        head_weight,
    )
    depth_rows = jnp.pad(depth_grad.reshape(128, 147), ((0, 0), (0, 8 * 128 - 147)))
    grads = jnp.concatenate(
        [expand_grad.reshape(128, 36, 128), reduce_grad.reshape(128, 36, 128), depth_rows.reshape(128, 8, 128)],
        axis=1,
    ).astype(jnp.bfloat16)
    shares = reduce_scatter(grads.reshape(4, 2, 4, 4, ROWS, 128))
    return (
        tile_out,
        feature,
        shares[0:36].reshape(-1),
        shares[36:72].reshape(-1),
        shares[72:80].reshape(-1)[:147],
    )


def solution(mesh):
    return jax.shard_map(
        on_device,
        mesh=mesh,
        in_specs=(
            P(("dp", "group"), None, None, None),
            P(None, ("dp", "group")),
            P("dp"),
            P(None, "group", None),
            P(),
            P(),
            P(),
            P(),
            P(),
            P(),
            P(),
            P(),
            P(),
            P(),
            P(),
            P(),
            P(),
            P("dp", None),
        ),
        out_specs=(
            P(("dp", "group"), None, None, None),
            P("dp", None),
            P(("dp", "group")),
            P(("dp", "group")),
            P(("dp", "group")),
        ),
        check_vma=False,
    )
```

```python
import math

import jax
import jax.numpy as jnp
from jax import lax
from jax.experimental import pallas as pl
from jax.experimental.pallas import tpu as pltpu
from jax.sharding import PartitionSpec as P

PROC = 4
EPSILON = 1e-06
HALF_ROOT = 0.7071067811865476
INV_ROOT_TAU = 0.3989422804014327
MESH = pl.DeviceIdType.MESH

WIDE = 14
STEP_U = 4
ROWS_STEP = STEP_U * 64
CHUNK = STEP_U * 16


def nt_dot(left, right):
    return lax.dot_general(left, right, (((1,), (1,)), ((), ())), preferred_element_type=jnp.float32)


def tn_dot(left, right):
    return lax.dot_general(left, right, (((0,), (0,)), ((), ())), preferred_element_type=jnp.float32)


def gelu_and_slope(pre):
    phi = 0.5 + 0.5 * lax.erf(pre * HALF_ROOT)
    return pre * phi, phi + pre * (INV_ROOT_TAU * jnp.exp(-0.5 * (pre * pre)))


def forward_kernel(routing, *refs):
    held, refs = refs[:11], refs[11:]
    forward_body(routing, held, *refs)


def forward_body(routing, held, tile_out, embed, cells, unit, inv_std, normed, hidden, slope, head_slope,
                   depth, section, embed_sum, arrived0, arrived1, arrived2, arrived3, leaving, send, recv, fetch, *local):
    f32, bf16 = jnp.float32, jnp.bfloat16
    dp, group = lax.axis_index("dp"), lax.axis_index("group")
    peers = [lax.rem(dp + k, 8) for k in range(8)]
    fetches = [pltpu.make_async_copy(a, b, fetch.at[i]) for i, (a, b) in enumerate(zip(held, local))]
    for copy in fetches:
        copy.start()
    tiles, depth_kernel, depth_bias, gain, shift, expand, expand_bias, reduce, reduce_bias, scale, head = local
    barrier = pltpu.get_barrier_semaphore()
    for to in peers[1:]:
        pl.semaphore_signal(barrier, inc=1, device_id=(to, group), device_id_type=MESH)

    def slot_for(to):
        found = 0
        for s in range(1, 8):
            local = routing[dp, 0, s] - to * PROC
            found = jnp.where((local >= 0) & (local < PROC), s, found)
        return found

    slots = [slot_for(to) for to in peers]
    source = []
    for q in range(PROC):
        found = -1
        for d in range(8):
            for s in range(8):
                found = jnp.where(routing[d, 0, s] == dp * PROC + q, d, found)
        source.append(found)

    arrived = (arrived0, arrived1, arrived2, arrived3)

    def chunk_copy(c, k):
        return pltpu.make_async_remote_copy(
            src_ref=leaving.at[k - 1, pl.ds(c * CHUNK, CHUNK)], dst_ref=arrived[c].at[dp], send_sem=send.at[c * 7 + k - 1],
            recv_sem=recv.at[c * 7 + k - 1], device_id=(peers[k], group), device_id_type=MESH)

    pl.semaphore_wait(barrier, 7)
    fetches[0].wait()

    for c in range(4):
        rows = pl.ds(c * CHUNK, CHUNK)
        for k in (4, 5, 3, 2, 6, 1, 7):
            leaving[k - 1, rows, :] = tiles[slots[k], rows, :]
            chunk_copy(c, k).start()
        arrived[c][dp] = tiles[slots[0], rows, :]
    edge = 3 * WIDE * 8
    cells[:, 0:edge] = jnp.zeros((3, edge, 128), f32)
    cells[:, edge + 16 * WIDE * 8:] = jnp.zeros((3, edge, 128), f32)
    zeros3 = jnp.zeros((3, 128), f32)

    def fill(c, i):
        u = c * STEP_U + i
        base = (u + 3) * (WIDE * 8)
        for q in range(PROC):
            src = source[q]
            row = arrived[c][jnp.maximum(src, 0), i * 16:i * 16 + 16, :].astype(f32)
            row = jnp.where(src >= 0, row, 0.0)
            for block in range(3):
                lanes = slice(block * 128, block * 128 + 128)
                cells[block, pl.ds(base + q * 2, 3, stride=8), :] = zeros3
                cells[block, pl.ds(base + 24 + q * 2, 11, stride=8), :] = row[0:11, lanes]
                cells[block, pl.ds(base + q * 2 + 1, 11, stride=8), :] = row[5:16, lanes]
                cells[block, pl.ds(base + 88 + q * 2 + 1, 3, stride=8), :] = zeros3

    def land(c):
        for k in range(1, 8):
            chunk_copy(c, k).wait_recv()
        for i in range(STEP_U):
            fill(c, i)

    for copy in fetches[1:]:
        copy.wait()
    land(0)
    embed_sum[...] = jnp.zeros((6, 8, 128), f32)

    def step(n, carry):
        start = pl.multiple_of(n * ROWS_STEP, ROWS_STEP)

        for c in range(1, 4):
            @pl.when(n == c - 1)
            def _():
                land(c)

        for block in range(3):
            lanes = pl.ds(block * 128, 128)
            for part in range(STEP_U // 2):
                acc = [jnp.zeros((8, 8, 128), f32) + depth_bias[lanes].reshape(1, 1, 128) for _ in range(2)]
                for a in range(8):
                    first = pl.multiple_of((n * STEP_U + part * 2 + a) * (WIDE * 8), 8)
                    x = cells[block, pl.ds(first, WIDE * 8), :].reshape(WIDE, 8, 128)
                    for i in range(2):
                        if 0 <= a - i < 7:
                            for b in range(7):
                                acc[i] = acc[i] + depth_kernel[pl.ds((a - i) * 7 + b, 1), lanes].reshape(1, 1, 128) * x[b:b + 8]
                for i in range(2):
                    depth[pl.ds((part * 2 + i) * 64, 64), lanes] = acc[i].reshape(64, 128)
        value = depth[...]
        centred = value - jnp.mean(value, axis=1, keepdims=True)
        inv = lax.rsqrt(jnp.mean(centred * centred, axis=1, keepdims=True) + EPSILON)
        z = centred * inv
        unit[pl.ds(start, ROWS_STEP), :] = z
        inv_std[pl.ds(start, ROWS_STEP), :] = jnp.broadcast_to(inv, (ROWS_STEP, 128))
        norm = (z * gain[...].reshape(1, 384) + shift[...].reshape(1, 384)).astype(bf16)
        normed[pl.ds(start, ROWS_STEP), :] = norm
        for m in range(6):
            cols = pl.ds(m * 256, 256)
            pre = jnp.dot(norm, expand[:, cols], preferred_element_type=f32) + expand_bias[cols].reshape(1, 256)
            act, grad = gelu_and_slope(pre)
            hidden[pl.ds(start, ROWS_STEP), cols] = act.astype(bf16)
            slope[pl.ds(start, ROWS_STEP), cols] = grad.astype(bf16)
        mlp = jnp.dot(hidden[pl.ds(start, ROWS_STEP), :], reduce[...], preferred_element_type=f32) + reduce_bias[...].reshape(1, 384)
        mlp = mlp * scale[...].reshape(1, 384)
        for i in range(STEP_U):
            first = pl.multiple_of((n * STEP_U + i + 3) * (WIDE * 8) + 24, 8)
            for block in range(3):
                section[block, pl.ds(i * 64, 64), :] = cells[block, pl.ds(first, 64), :] + mlp[i * 64:(i + 1) * 64, block * 128:block * 128 + 128]
        sec = jnp.concatenate([section[block] for block in range(3)], axis=1).astype(bf16)
        for m in range(3):
            cols = pl.ds(m * 256, 256)
            act, grad = gelu_and_slope(jnp.dot(sec, head[:, cols], preferred_element_type=f32))
            head_slope[pl.ds(start, ROWS_STEP), cols] = grad.astype(bf16)
            act = jnp.sum(act.reshape(STEP_U * 8, 8, 256), axis=0)
            for half in range(2):
                embed_sum[m * 2 + half] = embed_sum[m * 2 + half] + act[:, half * 128:half * 128 + 128]
        for i in range(STEP_U):
            for q in range(PROC):
                for block in range(3):
                    left = section[block, pl.ds(i * 64 + q * 2, 8, stride=8), :]
                    right = section[block, pl.ds(i * 64 + q * 2 + 1, 8, stride=8), :]
                    row = jnp.where(source[q] >= 0, jnp.concatenate([left, right], axis=0), 0.0)
                    tile_out[q, pl.ds(pl.multiple_of((n * STEP_U + i) * 16, 16), 16), pl.ds(block * 128, 128)] = row.astype(bf16)
        return carry

    lax.fori_loop(0, 16 // STEP_U, step, 0)
    means = [
        (embed_sum[block, pl.ds(0, 4, stride=2), :] + embed_sum[block, pl.ds(1, 4, stride=2), :]) * (1.0 / 256.0)
        for block in range(6)
    ]
    embed[...] = jnp.concatenate(means + [jnp.zeros((8, 128), f32)], axis=0).astype(bf16)

    for c in range(4):
        for k in range(1, 8):
            chunk_copy(c, k).wait_send()


def forward(routing, *arrays):
    f32, bf16 = jnp.float32, jnp.bfloat16
    vm = pl.BlockSpec(memory_space=pltpu.VMEM)
    out = lambda shape, kind: jax.ShapeDtypeStruct(shape, kind)
    return pl.pallas_call(
        forward_kernel,
        out_shape=(out((PROC, 256, 384), bf16), out((32, 128), bf16), out((3, 22 * WIDE * 8, 128), f32),
                   out((1024, 384), f32), out((1024, 128), f32), out((1024, 384), bf16),
                   out((1024, 1536), bf16), out((1024, 1536), bf16), out((1024, 768), bf16)),
        in_specs=[pl.BlockSpec(memory_space=pltpu.SMEM)] + [pl.BlockSpec(memory_space=pl.ANY)] * 11,
        out_specs=(vm,) * 9,
        scratch_shapes=[pltpu.VMEM((ROWS_STEP, 384), f32), pltpu.VMEM((3, ROWS_STEP, 128), f32), pltpu.VMEM((6, 8, 128), f32),
                        *[pltpu.VMEM((8, CHUNK, 384), bf16) for _ in range(4)], pltpu.VMEM((7, 256, 384), bf16),
                        pltpu.SemaphoreType.DMA((28,)), pltpu.SemaphoreType.DMA((28,)), pltpu.SemaphoreType.DMA((11,))]
        + [pltpu.VMEM(a.shape, a.dtype) for a in arrays],
        compiler_params=pltpu.CompilerParams(collective_id=3, has_side_effects=True, vmem_limit_bytes=60 * 2**20),
        name="block_forward",
    )(routing, *arrays)


def backward_kernel(embed_grad, cells, unit, inv_std, normed, hidden, slope, head_slope, gain, expand, reduce, scale,
                    head, shares, grad_mlp, grad_pre, depthwise, flat, flat2, taps):
    f32, bf16 = jnp.float32, jnp.bfloat16
    eg_row = jnp.concatenate([embed_grad[8 * block:8 * block + 8] for block in range(6)], axis=1) * (1.0 / 256.0)

    def first(n, carry):
        rows = pl.ds(pl.multiple_of(n * 256, 256), 256)
        gh = (eg_row[None] * head_slope[rows, :].astype(f32).reshape(32, 8, 768)).reshape(256, 768).astype(bf16)
        grad_mlp[rows, :] = (scale[...].reshape(1, 384) * nt_dot(gh, head[...])).astype(bf16)
        return carry

    lax.fori_loop(0, 4, first, 0)

    for m in range(6):
        cols = pl.ds(m * 256, 256)
        for n in range(4):
            rows = pl.ds(n * 256, 256)
            gp = nt_dot(grad_mlp[rows, :], reduce[cols, :]) * slope[rows, cols].astype(f32)
            grad_pre[rows, cols] = gp.astype(bf16)
        eg_m = tn_dot(normed[...], grad_pre[:, cols])
        for l in range(2):
            flat[pl.ds(m * 2 + l, 384, stride=12), :] = eg_m[:, l * 128:(l + 1) * 128]
    for m in range(6):
        rg_m = tn_dot(hidden[:, pl.ds(m * 256, 256)], grad_mlp[...])
        for l in range(3):
            flat2[pl.ds(m * 768 + l, 256, stride=3), :] = rg_m[:, l * 128:(l + 1) * 128]

    def second(n, carry):
        rows = pl.ds(pl.multiple_of(n * 256, 256), 256)
        w = nt_dot(grad_pre[rows, :], expand[...]) * gain[...].reshape(1, 384)
        z = unit[rows, :]
        inv = jnp.concatenate([inv_std[rows, :]] * 3, axis=1)
        depthwise[rows, :] = inv * (w - jnp.mean(w, axis=1, keepdims=True) - z * jnp.mean(w * z, axis=1, keepdims=True))
        return carry

    lax.fori_loop(0, 4, second, 0)

    for block in range(3):
        lanes = pl.ds(block * 128, 128)
        for a in range(7):
            def row(u, acc):
                g = depthwise[pl.ds(pl.multiple_of(u * 64, 64), 64), lanes].reshape(8, 8, 128)
                x = cells[block, pl.ds(pl.multiple_of((u + a) * (WIDE * 8), 8), WIDE * 8), :].reshape(WIDE, 8, 128)
                return tuple(acc[b] + jnp.sum(g * x[b:b + 8], axis=0) for b in range(7))
            acc = lax.fori_loop(0, 16, row, tuple(jnp.zeros((8, 128), f32) for _ in range(7)))
            for b in range(7):
                taps[pl.ds((a * 7 + b) * 3 + block, 1), :] = jnp.sum(acc[b], axis=0, keepdims=True)

    lane = lax.broadcasted_iota(jnp.int32, (8, 128), 1)
    flat2[4608:] = jnp.zeros((8, 128), f32)
    taps[147:] = jnp.zeros((13, 128), f32)
    for i in range(128):
        turn = (147 * i) % 128
        near = taps[pl.ds(147 * i // 128, 8), :]
        near = pltpu.roll(near, (128 - turn) % 128, 1) if turn else near
        near = jnp.where(lane < 128 - turn, near, pltpu.roll(near, 7, 0))
        shares[i, 0:32] = flat[pl.ds(i * 36, 32), :].astype(bf16)
        shares[i, 32:48] = jnp.concatenate([flat[pl.ds(i * 36 + 32, 4), :], near[0:4], flat2[pl.ds(i * 36, 8), :]], axis=0).astype(bf16)
        shares[i, 48:80] = flat2[pl.ds(i * 36 + 8, 32), :].astype(bf16)


def backward(embed_grad, acts, gain, expand, reduce, scale, head):
    f32, bf16 = jnp.float32, jnp.bfloat16
    vm = pl.BlockSpec(memory_space=pltpu.VMEM)
    row = lambda v: v
    return pl.pallas_call(
        backward_kernel,
        out_shape=jax.ShapeDtypeStruct((128, 80, 128), bf16),
        in_specs=[vm] * 13,
        out_specs=vm,
        scratch_shapes=[pltpu.VMEM((1024, 384), bf16), pltpu.VMEM((1024, 1536), bf16),
                        pltpu.VMEM((1024, 384), f32), pltpu.VMEM((4608, 128), f32), pltpu.VMEM((4616, 128), f32),
                        pltpu.VMEM((160, 128), f32)],
        compiler_params=pltpu.CompilerParams(vmem_limit_bytes=40 * 2**20),
        name="block_backward",
    )(embed_grad, *acts, row(gain), expand, reduce, row(scale), head)


def slide_kernel(count, routing, positions, embeds, taps, weight, bias, cot, feature, embed_grad,
                 emb_all, rows_mine, rows_all, wide, grad_wide, grad_mine, grad_all,
                 send1, recv1, send2, recv2, send3, recv3):
    f32, bf16, i32 = jnp.float32, jnp.bfloat16, jnp.int32
    dp, group = lax.axis_index("dp"), lax.axis_index("group")
    barrier = pltpu.get_barrier_semaphore()
    dp_peers = [lax.rem(dp + k, 8) for k in range(1, 8)]
    group_peers = [lax.rem(group + k, 16) for k in range(1, 16)]
    for to in dp_peers:
        pl.semaphore_signal(barrier, inc=1, device_id=(to, group), device_id_type=MESH)
    for to in group_peers:
        pl.semaphore_signal(barrier, inc=1, device_id=(dp, to), device_id_type=MESH)
    pl.semaphore_wait(barrier, 22)

    def over_dp(source, landing, send, recv):
        copies = []
        for k, to in enumerate(dp_peers):
            cp = pltpu.make_async_remote_copy(src_ref=source, dst_ref=landing.at[dp], send_sem=send.at[k], recv_sem=recv.at[k], device_id=(to, group), device_id_type=MESH)
            cp.start()
            copies.append(cp)
        landing[dp] = source[...]
        return copies

    def iota(shape, axis):
        return lax.broadcasted_iota(i32, shape, axis)

    copies1 = over_dp(embeds, emb_all, send1, recv1)
    places = count[0]

    row = iota((48, 128), 0)
    slot, block = row & 7, row >> 3
    channel = jnp.where(block >= 3, block - 3, block) * 128 + iota((48, 128), 1)
    spot = jnp.zeros((48, 128), i32)
    for s in range(8):
        spot = jnp.where(slot == s, jnp.where(block >= 3, positions[1, s], positions[0, s]), spot)
    frequency = jnp.exp((channel - (channel & 1)).astype(f32) * (-math.log(10000.0) / 384))
    angle = spot.astype(f32) * frequency
    pos_code = jnp.where((channel & 1) == 0, jnp.sin(angle), jnp.cos(angle))
    here = slot * 16 + group < places

    pick_row, pick_col = iota((48, 32), 0), iota((48, 32), 1)
    goes_to = jnp.full((48, 32), -1, i32)
    for s in range(8):
        goes_to = jnp.where((pick_row & 7) == s, routing[dp, 0, s], goes_to)
    goes_to = jnp.where((pick_row >> 3) == (pick_col >> 2), goes_to, -1)
    grad_row, grad_col = iota((48, 48), 0), iota((48, 48), 1)
    grad_place = jnp.where((grad_row >> 3) == (grad_col >> 3), dp * PROC + ((grad_row & 7) >> 1), -2)
    grad_picks = []
    for d in range(8):
        routed = jnp.full((48, 48), -1, i32)
        for s in range(8):
            routed = jnp.where((grad_col & 7) == s, routing[d, 0, s], routed)
        grad_picks.append(jnp.where(routed == grad_place, 1.0, 0.0).astype(bf16))

    for cp in copies1:
        cp.wait_recv()
    own = pos_code
    for e in range(8):
        pick = jnp.where(goes_to == e * PROC + (pick_col & 3), 1.0, 0.0).astype(bf16)
        own = own + jnp.dot(pick, emb_all[e], preferred_element_type=f32)
    rows_mine[...] = jnp.where(here, own, 0.0).astype(bf16)
    copies2 = []
    for k, to in enumerate(group_peers):
        cp = pltpu.make_async_remote_copy(src_ref=rows_mine, dst_ref=rows_all.at[group], send_sem=send2.at[k], recv_sem=recv2.at[k], device_id=(dp, to), device_id_type=MESH)
        cp.start()
        copies2.append(cp)
    rows_all[group] = rows_mine[...]
    for cp in copies2:
        cp.wait_recv()

    first, last = slot[0:8] == 0, slot[0:8] == 7

    def widen(block_rows, target):
        target[9:25] = block_rows
        for g in range(9):
            target[g] = jnp.where(first, 0.0, pltpu.roll(block_rows[g + 7], 1, 0))
            target[25 + g] = jnp.where(last, 0.0, pltpu.roll(block_rows[g], 7, 0))

    mixed = []
    for b in range(6):
        rows = rows_all[:, b * 8:b * 8 + 8, :].astype(f32)
        widen(rows, wide)
        total = rows
        for k in range(7):
            total = total + taps[pl.ds(k, 1), pl.ds(b * 128, 128)].reshape(1, 1, 128) * wide[3 * k:3 * k + 16]
        mixed.append(total.reshape(128, 128).astype(bf16))
    mixed = jnp.concatenate(mixed, axis=1)
    pre = jnp.dot(mixed, weight[...], preferred_element_type=f32) + bias[...].reshape(1, 768)
    seq_row = iota((128, 768), 0)
    share = jnp.where((seq_row & 7) * 16 + (seq_row >> 3) < places, 1.0, 0.0) / places.astype(f32)
    phi = 0.5 * (1.0 + lax.erf(pre * HALF_ROOT))
    slope = phi + pre * INV_ROOT_TAU * jnp.exp(-0.5 * pre * pre)
    grad_agg = (cot[...] * share * slope).astype(bf16)
    grad_mixed = lax.dot_general(grad_agg, weight[...], (((1,), (1,)), ((), ())), preferred_element_type=f32)
    grad_rows = []
    for b in range(6):
        widen(grad_mixed[:, b * 128:b * 128 + 128].reshape(16, 8, 128), grad_wide)
        total = grad_wide[9 + group]
        for k in range(7):
            total = total + taps[pl.ds(k, 1), pl.ds(b * 128, 128)] * grad_wide[group + 18 - 3 * k]
        grad_rows.append(total)
    grad_mine[...] = jnp.where(here, jnp.concatenate(grad_rows, axis=0), 0.0).astype(bf16)
    copies3 = over_dp(grad_mine, grad_all, send3, recv3)
    feature[...] = jnp.sum(pre * phi * share, axis=0, keepdims=True)
    for cp in copies3:
        cp.wait_recv()
    total = jnp.zeros((48, 128), f32)
    for d in range(8):
        total = total + jnp.dot(grad_picks[d], grad_all[d], preferred_element_type=f32)
    embed_grad[...] = total
    for cp in copies1 + copies2 + copies3:
        cp.wait_send()


def slide_step(count, routing, positions, embeds, taps, weight, bias, cot):
    f32, bf16 = jnp.float32, jnp.bfloat16
    vm = pl.BlockSpec(memory_space=pltpu.VMEM)
    sm = pl.BlockSpec(memory_space=pltpu.SMEM)
    sem = lambda n: pltpu.SemaphoreType.DMA((n,))
    return pl.pallas_call(
        slide_kernel,
        out_shape=(jax.ShapeDtypeStruct((1, 768), f32), jax.ShapeDtypeStruct((48, 128), f32)),
        in_specs=[sm] * 3 + [vm] * 5,
        out_specs=(vm, vm),
        scratch_shapes=[
            pltpu.VMEM((8, 32, 128), bf16), pltpu.VMEM((48, 128), bf16), pltpu.VMEM((16, 48, 128), bf16),
            pltpu.VMEM((34, 8, 128), f32), pltpu.VMEM((34, 8, 128), f32),
            pltpu.VMEM((48, 128), bf16), pltpu.VMEM((8, 48, 128), bf16),
            sem(7), sem(7), sem(15), sem(15), sem(7), sem(7),
        ],
        compiler_params=pltpu.CompilerParams(collective_id=2, has_side_effects=True, vmem_limit_bytes=16 * 2**20),
        name="slide_step",
    )(count, routing, positions, embeds, taps, weight, bias, cot)


PARTS = (32, 32, 16)
ORDERS = ("yxz", "xzy", "zyx")
ROWS = sum(PARTS)

def torus_place():
    dp, group = lax.axis_index("dp"), lax.axis_index("group")
    return {"y": lax.div(dp, 2), "c": lax.rem(dp, 2), "x": lax.div(group, 4), "z": lax.rem(group, 4)}

def torus_device(place, **moved):
    at = {**place, **moved}
    return (at["y"] * 2 + at["c"], at["x"] * 4 + at["z"])

def reduce_scatter_kernel(grads, out, core_in, s1, s2, s3, r1, r2, r3, core_send, core_recv, send, recv):
    place = torus_place()
    partner = torus_device(place, c=1 - place["c"])
    barrier = pltpu.get_barrier_semaphore()
    pl.semaphore_signal(barrier, inc=1, device_id=partner, device_id_type=MESH)
    for axis in "yxz":
        for k in (1, 2, 3):
            pl.semaphore_signal(barrier, inc=1, device_id=torus_device(place, **{axis: lax.rem(place[axis] + k, 4)}), device_id_type=MESH)
    pl.semaphore_wait(barrier, 10)

    core_copies = []
    for y in range(4):
        cp = pltpu.make_async_remote_copy(src_ref=grads.at[y, 1 - place["c"]], dst_ref=core_in.at[y], send_sem=core_send.at[y], recv_sem=core_recv.at[y], device_id=partner, device_id_type=MESH)
        cp.start()
        core_copies.append(cp)

    def start(stage, part, source, landing):
        axis = ORDERS[part][stage]
        made = []
        for k in (2, 1, 3):
            to = lax.rem(place[axis] + k, 4)
            cp = pltpu.make_async_remote_copy(src_ref=source.at[to], dst_ref=landing.at[k - 1], send_sem=send.at[stage * 9 + part * 3 + k - 1], recv_sem=recv.at[stage * 9 + part * 3 + k - 1], device_id=torus_device(place, **{axis: to}), device_id_type=MESH)
            cp.start()
            made.append(cp)
        return made

    f32 = jnp.float32
    for y in range(4):
        core_copies[y].wait_recv()
        for x in range(4):
            both = grads[y, place["c"], x].astype(f32) + core_in[y, x].astype(f32)
            both = both.astype(jnp.bfloat16)
            s1[0][y, x] = both[:, 0:32]
            s1[1][x, :, y] = both[:, 32:64]
            for z in range(4):
                s1[2][z, y, x] = both[z, 64:80]
    flying = [start(0, part, s1[part], r1[part]) for part in range(3)]
    flying2 = []
    for part in range(3):
        for cp in flying[part]:
            cp.wait_recv()
        mine = place[ORDERS[part][0]]
        for a in range(4):
            total = s1[part][mine, a].astype(f32)
            for k in range(3):
                total = total + r1[part][k, a].astype(f32)
            s2[part][a] = total.astype(jnp.bfloat16)
        flying2.append(start(1, part, s2[part], r2[part]))
    flying3 = []
    for part in range(3):
        for cp in flying2[part]:
            cp.wait_recv()
        mine = place[ORDERS[part][1]]
        total = s2[part][mine].astype(f32)
        for k in range(3):
            total = total + r2[part][k].astype(f32)
        s3[part][...] = total.astype(jnp.bfloat16)
        flying3.append(start(2, part, s3[part], r3[part]))
    base = 0
    for part in range(3):
        for cp in flying3[part]:
            cp.wait_recv()
        total = s3[part][place[ORDERS[part][2]]].astype(f32)
        for k in range(3):
            total = total + r3[part][k].astype(f32)
        out[base:base + PARTS[part]] = total
        base += PARTS[part]
    for cp in core_copies:
        cp.wait_send()
    for copies in flying + flying2 + flying3:
        for cp in copies:
            cp.wait_send()

def reduce_scatter(grads):
    bf16 = jnp.bfloat16
    buf = lambda *lead: [pltpu.VMEM(lead + (rows, 128), bf16) for rows in PARTS]
    return pl.pallas_call(
        reduce_scatter_kernel,
        out_shape=jax.ShapeDtypeStruct((ROWS, 128), jnp.float32),
        in_specs=[pl.BlockSpec(memory_space=pltpu.VMEM)],
        out_specs=pl.BlockSpec(memory_space=pltpu.VMEM),
        scratch_shapes=[
            pltpu.VMEM((4, 4, 4, ROWS, 128), bf16),
            buf(4, 4, 4), buf(4, 4), buf(4), buf(3, 4, 4), buf(3, 4), buf(3),
            pltpu.SemaphoreType.DMA((4,)), pltpu.SemaphoreType.DMA((4,)),
            pltpu.SemaphoreType.DMA((27,)), pltpu.SemaphoreType.DMA((27,)),
        ],
        compiler_params=pltpu.CompilerParams(collective_id=1, has_side_effects=True, vmem_limit_bytes=32 * 2**20),
        name="grad_reduce_scatter",
    )(grads)


def on_device(
    tile_maps,
    positions,
    counts,
    routing,
    depth_kernel,
    depth_bias,
    norm_gain,
    norm_shift,
    expand_weight,
    expand_bias,
    reduce_weight,
    reduce_bias,
    layer_scale,
    head_weight,
    slide_taps,
    slide_weight,
    slide_bias,
    cotangent,
):
    tile_out, embeds, *acts = forward(
        routing,
        tile_maps.reshape(8, 256, 384),
        depth_kernel,
        depth_bias,
        norm_gain,
        norm_shift,
        expand_weight,
        expand_bias,
        reduce_weight,
        reduce_bias,
        layer_scale,
        head_weight,
    )
    feature, embed_grad = slide_step(
        counts, routing, positions, embeds, slide_taps, slide_weight, slide_bias, cotangent
    )
    grads = backward(embed_grad, acts, norm_gain, expand_weight, reduce_weight, layer_scale, head_weight)
    shares = reduce_scatter(grads.reshape(4, 2, 4, 4, ROWS, 128))
    return (
        tile_out.reshape((PROC,) + tile_maps.shape[1:]),
        feature,
        shares[0:36].reshape(-1),
        shares[40:76].reshape(-1),
        shares[36:38].reshape(-1)[:147],
    )


def solution(mesh):
    return jax.shard_map(
        on_device,
        mesh=mesh,
        in_specs=(
            P(("dp", "group"), None, None, None),
            P(None, ("dp", "group")),
            P("dp"),
            P(None, "group", None),
            P(),
            P(),
            P(),
            P(),
            P(),
            P(),
            P(),
            P(),
            P(),
            P(),
            P(),
            P(),
            P(),
            P("dp", None),
        ),
        out_specs=(
            P(("dp", "group"), None, None, None),
            P("dp", None),
            P(("dp", "group")),
            P(("dp", "group")),
            P(("dp", "group")),
        ),
        check_vma=False,
    )
```

```python
import functools
import math
import types

import jax
import jax.numpy as jnp
from jax import lax
from jax.experimental import pallas as pl
from jax.experimental.pallas import tpu as pltpu
from jax.sharding import PartitionSpec as P

PROC = 4
EPSILON = 1e-06
HALF_ROOT = 0.7071067811865476
INV_ROOT_TAU = 0.3989422804014327
MESH = pl.DeviceIdType.MESH

WIDE = 14
STEP_U = 4
ROWS_STEP = STEP_U * 64
CHUNK = STEP_U * 16


def nt_dot(left, right):
    return lax.dot_general(left, right, (((1,), (1,)), ((), ())), preferred_element_type=jnp.float32)


def tn_dot(left, right):
    return lax.dot_general(left, right, (((0,), (0,)), ((), ())), preferred_element_type=jnp.float32)


def gelu_and_slope(pre):
    phi = 0.5 + 0.5 * lax.erf(pre * HALF_ROOT)
    return pre * phi, phi + pre * (INV_ROOT_TAU * jnp.exp(-0.5 * (pre * pre)))


def tile_sources(routing, dp):
    source = []
    for q in range(PROC):
        found = -1
        for d in range(8):
            for s in range(8):
                found = jnp.where(routing[d, 0, s] == dp * PROC + q, d, found)
        source.append(found)
    return source


def emit_tiles(ref, source):
    def tile_row(u, carry):
        for q in range(PROC):
            for block in range(3):
                left = ref.section[block, pl.ds(u * 64 + q * 2, 8, stride=8), :]
                right = ref.section[block, pl.ds(u * 64 + q * 2 + 1, 8, stride=8), :]
                row = jnp.where(source[q] >= 0, jnp.concatenate([left, right], axis=0), 0.0)
                ref.tile_out[q, pl.ds(pl.multiple_of(u * 16, 16), 16), pl.ds(block * 128, 128)] = row.astype(jnp.bfloat16)
        return carry

    lax.fori_loop(0, 16, tile_row, 0)


def forward(ref, dp, group):
    f32, bf16 = jnp.float32, jnp.bfloat16
    routing, tiles, leaving, send, recv = ref.routing, ref.tiles, ref.leaving, ref.tile_send, ref.tile_recv
    cells, section, embed_sum, depth = ref.cells, ref.section, ref.embed_sum, ref.depth
    peers = [lax.rem(dp + k, 8) for k in range(8)]

    def slot_for(to):
        found = 0
        for s in range(1, 8):
            local = routing[dp, 0, s] - to * PROC
            found = jnp.where((local >= 0) & (local < PROC), s, found)
        return found

    slots = [slot_for(to) for to in peers]
    source = tile_sources(routing, dp)

    arrived = (ref.arrived0, ref.arrived1, ref.arrived2, ref.arrived3)

    def chunk_copy(c, k):
        return pltpu.make_async_remote_copy(
            src_ref=leaving.at[k - 1, pl.ds(c * CHUNK, CHUNK)], dst_ref=arrived[c].at[dp], send_sem=send.at[c * 7 + k - 1],
            recv_sem=recv.at[c * 7 + k - 1], device_id=(peers[k], group), device_id_type=MESH)

    pl.semaphore_wait(pltpu.get_barrier_semaphore(), 22)
    ref.fetches[0].wait()

    for c in range(4):
        rows = pl.ds(c * CHUNK, CHUNK)
        for k in (4, 5, 3, 2, 6, 1, 7):
            leaving[k - 1, rows, :] = tiles[slots[k], rows, :]
            chunk_copy(c, k).start()
        arrived[c][dp] = tiles[slots[0], rows, :]
    edge = 3 * WIDE * 8
    cells[:, 0:edge] = jnp.zeros((3, edge, 128), f32)
    cells[:, edge + 16 * WIDE * 8:] = jnp.zeros((3, edge, 128), f32)
    zeros3 = jnp.zeros((3, 128), f32)

    def fill(c, i):
        u = c * STEP_U + i
        base = (u + 3) * (WIDE * 8)
        for q in range(PROC):
            src = source[q]
            row = arrived[c][jnp.maximum(src, 0), i * 16:i * 16 + 16, :].astype(f32)
            row = jnp.where(src >= 0, row, 0.0)
            for block in range(3):
                lanes = slice(block * 128, block * 128 + 128)
                cells[block, pl.ds(base + q * 2, 3, stride=8), :] = zeros3
                cells[block, pl.ds(base + 24 + q * 2, 11, stride=8), :] = row[0:11, lanes]
                cells[block, pl.ds(base + q * 2 + 1, 11, stride=8), :] = row[5:16, lanes]
                cells[block, pl.ds(base + 88 + q * 2 + 1, 3, stride=8), :] = zeros3

    def land(c):
        for k in range(1, 8):
            chunk_copy(c, k).wait_recv()
        for i in range(STEP_U):
            fill(c, i)

    for copy in ref.fetches[1:]:
        copy.wait()
    land(0)
    embed_sum[...] = jnp.zeros((6, 8, 128), f32)

    def step(n, carry):
        start = pl.multiple_of(n * ROWS_STEP, ROWS_STEP)

        for c in range(1, 4):
            @pl.when(n == c - 1)
            def _():
                land(c)

        for block in range(3):
            lanes = pl.ds(block * 128, 128)
            for part in range(STEP_U // 2):
                acc = [jnp.zeros((8, 8, 128), f32) + ref.depth_bias[lanes].reshape(1, 1, 128) for _ in range(2)]
                for a in range(8):
                    first = pl.multiple_of((n * STEP_U + part * 2 + a) * (WIDE * 8), 8)
                    x = cells[block, pl.ds(first, WIDE * 8), :].reshape(WIDE, 8, 128)
                    for i in range(2):
                        if 0 <= a - i < 7:
                            for b in range(7):
                                acc[i] = acc[i] + ref.depth_kernel[pl.ds((a - i) * 7 + b, 1), lanes].reshape(1, 1, 128) * x[b:b + 8]
                for i in range(2):
                    depth[pl.ds((part * 2 + i) * 64, 64), lanes] = acc[i].reshape(64, 128)
        value = depth[...]
        centred = value - jnp.mean(value, axis=1, keepdims=True)
        inv = lax.rsqrt(jnp.mean(centred * centred, axis=1, keepdims=True) + EPSILON)
        z = centred * inv
        ref.unit[pl.ds(start, ROWS_STEP), :] = z
        ref.inv_std[pl.ds(start, ROWS_STEP), :] = jnp.broadcast_to(inv, (ROWS_STEP, 128))
        norm = (z * ref.gain[...].reshape(1, 384) + ref.shift[...].reshape(1, 384)).astype(bf16)
        ref.normed[pl.ds(start, ROWS_STEP), :] = norm
        for m in range(6):
            cols = pl.ds(m * 256, 256)
            pre = jnp.dot(norm, ref.expand[:, cols], preferred_element_type=f32) + ref.expand_bias[cols].reshape(1, 256)
            act, grad = gelu_and_slope(pre)
            ref.hidden[pl.ds(start, ROWS_STEP), cols] = act.astype(bf16)
            ref.slope[pl.ds(start, ROWS_STEP), cols] = grad.astype(bf16)
        mlp = jnp.dot(ref.hidden[pl.ds(start, ROWS_STEP), :], ref.reduce[...], preferred_element_type=f32) + ref.reduce_bias[...].reshape(1, 384)
        mlp = mlp * ref.scale[...].reshape(1, 384)
        for i in range(STEP_U):
            first = pl.multiple_of((n * STEP_U + i + 3) * (WIDE * 8) + 24, 8)
            for block in range(3):
                section[block, pl.ds(pl.multiple_of(start + i * 64, 64), 64), :] = cells[block, pl.ds(first, 64), :] + mlp[i * 64:(i + 1) * 64, block * 128:block * 128 + 128]
        sec = jnp.concatenate([section[block, pl.ds(start, ROWS_STEP), :] for block in range(3)], axis=1).astype(bf16)
        for m in range(3):
            cols = pl.ds(m * 256, 256)
            act, grad = gelu_and_slope(jnp.dot(sec, ref.head[:, cols], preferred_element_type=f32))
            ref.head_slope[pl.ds(start, ROWS_STEP), cols] = grad.astype(bf16)
            act = jnp.sum(act.reshape(STEP_U * 8, 8, 256), axis=0)
            for half in range(2):
                embed_sum[m * 2 + half] = embed_sum[m * 2 + half] + act[:, half * 128:half * 128 + 128]
        return carry

    lax.fori_loop(0, 16 // STEP_U, step, 0)
    means = [
        (embed_sum[block, pl.ds(0, 4, stride=2), :] + embed_sum[block, pl.ds(1, 4, stride=2), :]) * (1.0 / 256.0)
        for block in range(6)
    ]
    ref.embed[...] = jnp.concatenate(means + [jnp.zeros((8, 128), f32)], axis=0).astype(bf16)

    def departed():
        for c in range(4):
            for k in range(1, 8):
                chunk_copy(c, k).wait_send()

    return departed


def slide_pass(ref, dp, group):
    routing, emb_all, rows_mine, rows_all = ref.routing, ref.emb_all, ref.rows_mine, ref.rows_all
    wide, grad_wide, grad_mine, grad_all = ref.wide, ref.grad_wide, ref.grad_mine, ref.grad_all
    f32, bf16, i32 = jnp.float32, jnp.bfloat16, jnp.int32
    dp_peers = [lax.rem(dp + k, 8) for k in range(1, 8)]
    group_peers = [lax.rem(group + k, 16) for k in range(1, 16)]

    def over_dp(source, landing, send, recv):
        copies = []
        for k, to in enumerate(dp_peers):
            cp = pltpu.make_async_remote_copy(src_ref=source, dst_ref=landing.at[dp], send_sem=send.at[k], recv_sem=recv.at[k], device_id=(to, group), device_id_type=MESH)
            cp.start()
            copies.append(cp)
        landing[dp] = source[...]
        return copies

    def iota(shape, axis):
        return lax.broadcasted_iota(i32, shape, axis)

    copies1 = over_dp(ref.embed, emb_all, ref.slide_send1, ref.slide_recv1)
    places = ref.count[0]

    row = iota((48, 128), 0)
    slot, block = row & 7, row >> 3
    channel = jnp.where(block >= 3, block - 3, block) * 128 + iota((48, 128), 1)
    spot = jnp.zeros((48, 128), i32)
    for s in range(8):
        spot = jnp.where(slot == s, jnp.where(block >= 3, ref.positions[1, s], ref.positions[0, s]), spot)
    frequency = jnp.exp((channel - (channel & 1)).astype(f32) * (-math.log(10000.0) / 384))
    angle = spot.astype(f32) * frequency
    pos_code = jnp.where((channel & 1) == 0, jnp.sin(angle), jnp.cos(angle))
    here = slot * 16 + group < places

    pick_row, pick_col = iota((48, 32), 0), iota((48, 32), 1)
    goes_to = jnp.full((48, 32), -1, i32)
    for s in range(8):
        goes_to = jnp.where((pick_row & 7) == s, routing[dp, 0, s], goes_to)
    goes_to = jnp.where((pick_row >> 3) == (pick_col >> 2), goes_to, -1)
    grad_row, grad_col = iota((48, 48), 0), iota((48, 48), 1)
    grad_place = jnp.where((grad_row >> 3) == (grad_col >> 3), dp * PROC + ((grad_row & 7) >> 1), -2)
    grad_picks = []
    for d in range(8):
        routed = jnp.full((48, 48), -1, i32)
        for s in range(8):
            routed = jnp.where((grad_col & 7) == s, routing[d, 0, s], routed)
        grad_picks.append(jnp.where(routed == grad_place, 1.0, 0.0).astype(bf16))

    emit_tiles(ref, tile_sources(routing, dp))
    for cp in copies1:
        cp.wait_recv()
    own = pos_code
    for e in range(8):
        pick = jnp.where(goes_to == e * PROC + (pick_col & 3), 1.0, 0.0).astype(bf16)
        own = own + jnp.dot(pick, emb_all[e], preferred_element_type=f32)
    rows_mine[...] = jnp.where(here, own, 0.0).astype(bf16)
    copies2 = []
    for k, to in enumerate(group_peers):
        cp = pltpu.make_async_remote_copy(src_ref=rows_mine, dst_ref=rows_all.at[group], send_sem=ref.slide_send2.at[k], recv_sem=ref.slide_recv2.at[k], device_id=(dp, to), device_id_type=MESH)
        cp.start()
        copies2.append(cp)
    rows_all[group] = rows_mine[...]
    for cp in copies2:
        cp.wait_recv()

    first, last = slot[0:8] == 0, slot[0:8] == 7

    def widen(block_rows, target):
        target[9:25] = block_rows
        for g in range(9):
            target[g] = jnp.where(first, 0.0, pltpu.roll(block_rows[g + 7], 1, 0))
            target[25 + g] = jnp.where(last, 0.0, pltpu.roll(block_rows[g], 7, 0))

    mixed = []
    for b in range(6):
        rows = rows_all[:, b * 8:b * 8 + 8, :].astype(f32)
        widen(rows, wide)
        total = rows
        for k in range(7):
            total = total + ref.slide_taps[pl.ds(k, 1), pl.ds(b * 128, 128)].reshape(1, 1, 128) * wide[3 * k:3 * k + 16]
        mixed.append(total.reshape(128, 128).astype(bf16))
    mixed = jnp.concatenate(mixed, axis=1)
    pre = jnp.dot(mixed, ref.slide_weight[...], preferred_element_type=f32) + ref.slide_bias[...].reshape(1, 768)
    seq_row = iota((128, 768), 0)
    share = jnp.where((seq_row & 7) * 16 + (seq_row >> 3) < places, 1.0, 0.0) / places.astype(f32)
    phi = 0.5 * (1.0 + lax.erf(pre * HALF_ROOT))
    slope = phi + pre * INV_ROOT_TAU * jnp.exp(-0.5 * pre * pre)
    grad_agg = (ref.cot[...] * share * slope).astype(bf16)
    grad_mixed = lax.dot_general(grad_agg, ref.slide_weight[...], (((1,), (1,)), ((), ())), preferred_element_type=f32)
    grad_rows = []
    for b in range(6):
        widen(grad_mixed[:, b * 128:b * 128 + 128].reshape(16, 8, 128), grad_wide)
        total = grad_wide[9 + group]
        for k in range(7):
            total = total + ref.slide_taps[pl.ds(k, 1), pl.ds(b * 128, 128)] * grad_wide[group + 18 - 3 * k]
        grad_rows.append(total)
    grad_mine[...] = jnp.where(here, jnp.concatenate(grad_rows, axis=0), 0.0).astype(bf16)
    copies3 = over_dp(grad_mine, grad_all, ref.slide_send3, ref.slide_recv3)
    ref.feature[...] = jnp.sum(pre * phi * share, axis=0, keepdims=True)
    for cp in copies3:
        cp.wait_recv()
    total = jnp.zeros((48, 128), f32)
    for d in range(8):
        total = total + jnp.dot(grad_picks[d], grad_all[d], preferred_element_type=f32)
    ref.embed_grad[...] = total
    return copies1 + copies2 + copies3


def backward_weights(ref):
    f32, bf16 = jnp.float32, jnp.bfloat16
    eg_row = jnp.concatenate([ref.embed_grad[8 * block:8 * block + 8] for block in range(6)], axis=1) * (1.0 / 256.0)

    def first(n, carry):
        rows = pl.ds(pl.multiple_of(n * 256, 256), 256)
        gh = (eg_row[None] * ref.head_slope[rows, :].astype(f32).reshape(32, 8, 768)).reshape(256, 768).astype(bf16)
        ref.grad_mlp[rows, :] = (ref.scale[...].reshape(1, 384) * nt_dot(gh, ref.head[...])).astype(bf16)
        return carry

    lax.fori_loop(0, 4, first, 0)

    for m in range(6):
        cols = pl.ds(m * 256, 256)
        for n in range(4):
            rows = pl.ds(n * 256, 256)
            gp = nt_dot(ref.grad_mlp[rows, :], ref.reduce[cols, :]) * ref.slope[rows, cols].astype(f32)
            ref.grad_pre[rows, cols] = gp.astype(bf16)
        eg_m = tn_dot(ref.normed[...], ref.grad_pre[:, cols])
        for l in range(2):
            ref.flat[pl.ds(m * 2 + l, 384, stride=12), :] = eg_m[:, l * 128:(l + 1) * 128]
    for m in range(6):
        rg_m = tn_dot(ref.hidden[:, pl.ds(m * 256, 256)], ref.grad_mlp[...])
        for l in range(3):
            ref.flat2[pl.ds(m * 768 + l, 256, stride=3), :] = rg_m[:, l * 128:(l + 1) * 128]

    ref.flat2[4608:] = jnp.zeros((8, 128), f32)

    def pack(i, carry):
        ref.shares[i, 0:32] = ref.flat[pl.ds(i * 36, 32), :].astype(bf16)
        ref.shares[i, 32:48] = jnp.concatenate(
            [ref.flat[pl.ds(i * 36 + 32, 4), :], jnp.zeros((4, 128), f32), ref.flat2[pl.ds(i * 36, 8), :]], axis=0
        ).astype(bf16)
        ref.shares[i, 48:80] = ref.flat2[pl.ds(i * 36 + 8, 32), :].astype(bf16)
        return carry

    lax.fori_loop(0, 128, pack, 0)


def backward_norm(ref):
    f32, bf16 = jnp.float32, jnp.bfloat16

    def second(n, carry):
        rows = pl.ds(pl.multiple_of(n * 256, 256), 256)
        w = nt_dot(ref.grad_pre[rows, :], ref.expand[...]) * ref.gain[...].reshape(1, 384)
        z = ref.unit[rows, :]
        inv = jnp.concatenate([ref.inv_std[rows, :]] * 3, axis=1)
        ref.depthwise[rows, :] = inv * (w - jnp.mean(w, axis=1, keepdims=True) - z * jnp.mean(w * z, axis=1, keepdims=True))
        return carry

    lax.fori_loop(0, 4, second, 0)


def backward_depth(ref):
    f32 = jnp.float32
    ref.taps[147:] = jnp.zeros((21, 128), f32)
    for block in range(3):
        lanes = pl.ds(block * 128, 128)
        for a in range(7):
            def row(u, acc):
                g = ref.depthwise[pl.ds(pl.multiple_of(u * 64, 64), 64), lanes].reshape(8, 8, 128)
                x = ref.cells[block, pl.ds(pl.multiple_of((u + a) * (WIDE * 8), 8), WIDE * 8), :].reshape(WIDE, 8, 128)
                return tuple(acc[b] + jnp.sum(g * x[b:b + 8], axis=0) for b in range(7))
            acc = lax.fori_loop(0, 16, row, tuple(jnp.zeros((8, 128), f32) for _ in range(7)))
            for b in range(7):
                ref.taps[pl.ds((a * 7 + b) * 3 + block, 1), :] = jnp.sum(acc[b], axis=0, keepdims=True)


def depth_exchange(ref, dp, group):
    f32, bf16 = jnp.float32, jnp.bfloat16
    copies = []
    for k in range(1, 8):
        to = lax.rem(dp + k, 8)
        ref.tap_leaving[k - 1] = ref.taps[pl.ds(lax.div(147 * to, 8), 32), :].astype(bf16)
        cp = pltpu.make_async_remote_copy(src_ref=ref.tap_leaving.at[k - 1], dst_ref=ref.tap_arrived.at[k - 1], send_sem=ref.tap_send.at[k - 1], recv_sem=ref.tap_recv.at[k - 1], device_id=(to, group), device_id_type=MESH)
        cp.start()
        copies.append(cp)
    yield
    total = ref.taps[pl.ds(lax.div(147 * dp, 8), 32), :]
    for cp in copies:
        cp.wait_recv()
    for k in range(7):
        total = total + ref.tap_arrived[k].astype(f32)
    ref.tap_mine[...] = total.astype(bf16)
    for k in range(1, 16):
        to = lax.rem(group + k, 16)
        cp = pltpu.make_async_remote_copy(src_ref=ref.tap_mine, dst_ref=ref.tap_group.at[k - 1], send_sem=ref.tap_send.at[6 + k], recv_sem=ref.tap_recv.at[6 + k], device_id=(dp, to), device_id_type=MESH)
        cp.start()
        copies.append(cp)
    yield
    for cp in copies[7:]:
        cp.wait_recv()
    for k in range(15):
        total = total + ref.tap_group[k].astype(f32)
    ref.tap_sum[...] = total
    begin = 147 * (16 * dp + group)
    row = lax.div(begin, 128) - lax.div(147 * dp, 8)
    turn = lax.rem(begin, 128)
    near = pltpu.roll(ref.tap_sum[pl.ds(row, 8), :], 128 - turn, 1)
    lane = lax.broadcasted_iota(jnp.int32, (8, 128), 1)
    ref.depth_out[...] = jnp.where(lane < 128 - turn, near, pltpu.roll(near, 7, 0))
    for cp in copies:
        cp.wait_send()


PARTS = (32, 32, 16)
ORDERS = ("yxz", "xzy", "zyx")
ROWS = sum(PARTS)

def torus_place():
    dp, group = lax.axis_index("dp"), lax.axis_index("group")
    return {"y": lax.div(dp, 2), "c": lax.rem(dp, 2), "x": lax.div(group, 4), "z": lax.rem(group, 4)}

def torus_device(place, **moved):
    at = {**place, **moved}
    return (at["y"] * 2 + at["c"], at["x"] * 4 + at["z"])

def share_exchange(ref):
    place = torus_place()
    partner = torus_device(place, c=1 - place["c"])
    core_in, core_send, core_recv, send, recv = ref.core_in, ref.core_send, ref.core_recv, ref.share_send, ref.share_recv
    s1, s2, s3, r1, r2, r3 = ref.s1, ref.s2, ref.s3, ref.r1, ref.r2, ref.r3
    core_copies = []
    for y in range(4):
        cp = pltpu.make_async_remote_copy(src_ref=ref.shares.at[pl.ds(pl.multiple_of((y * 2 + 1 - place["c"]) * 16, 16), 16)], dst_ref=core_in.at[y], send_sem=core_send.at[y], recv_sem=core_recv.at[y], device_id=partner, device_id_type=MESH)
        cp.start()
        core_copies.append(cp)

    def start(stage, part, source, landing):
        axis = ORDERS[part][stage]
        made = []
        for k in (2, 1, 3):
            to = lax.rem(place[axis] + k, 4)
            cp = pltpu.make_async_remote_copy(src_ref=source.at[to], dst_ref=landing.at[k - 1], send_sem=send.at[stage * 9 + part * 3 + k - 1], recv_sem=recv.at[stage * 9 + part * 3 + k - 1], device_id=torus_device(place, **{axis: to}), device_id_type=MESH)
            cp.start()
            made.append(cp)
        return made

    yield
    f32 = jnp.float32
    for y in range(4):
        core_copies[y].wait_recv()
        for x in range(4):
            both = ref.shares[pl.ds((y * 2 + place["c"]) * 16 + x * 4, 4)].astype(f32) + core_in[y, x * 4:x * 4 + 4].astype(f32)
            both = both.astype(jnp.bfloat16)
            s1[0][y, x] = both[:, 0:32]
            s1[1][x, :, y] = both[:, 32:64]
            for z in range(4):
                s1[2][z, y, x] = both[z, 64:80]
    flying = [start(0, part, s1[part], r1[part]) for part in range(3)]
    yield
    flying2 = []
    for part in range(3):
        for cp in flying[part]:
            cp.wait_recv()
        mine = place[ORDERS[part][0]]
        for a in range(4):
            total = s1[part][mine, a].astype(f32)
            for k in range(3):
                total = total + r1[part][k, a].astype(f32)
            s2[part][a] = total.astype(jnp.bfloat16)
        flying2.append(start(1, part, s2[part], r2[part]))
    yield
    flying3 = []
    for part in range(3):
        for cp in flying2[part]:
            cp.wait_recv()
        mine = place[ORDERS[part][1]]
        total = s2[part][mine].astype(f32)
        for k in range(3):
            total = total + r2[part][k].astype(f32)
        s3[part][...] = total.astype(jnp.bfloat16)
        flying3.append(start(2, part, s3[part], r3[part]))
    yield
    base = 0
    for part in range(3):
        for cp in flying3[part]:
            cp.wait_recv()
        total = s3[part][place[ORDERS[part][2]]].astype(f32)
        for k in range(3):
            total = total + r3[part][k].astype(f32)
        ref.share_sum[base:base + PARTS[part]] = total
        base += PARTS[part]
    ref.expand_out[...] = ref.share_sum[0:36]
    ref.reduce_out[...] = ref.share_sum[40:76]
    for cp in core_copies:
        cp.wait_send()
    for copies in flying + flying2 + flying3:
        for cp in copies:
            cp.wait_send()


SCALARS = ("count", "routing", "positions")
FETCHED = ("tiles", "depth_kernel", "depth_bias", "gain", "shift", "expand", "expand_bias", "reduce", "reduce_bias",
           "scale", "head", "slide_taps", "slide_weight", "slide_bias", "cot")
RESULTS = ("tile_out", "feature", "expand_out", "reduce_out", "depth_out")


def scratch_list(arrays):
    f32, bf16 = jnp.float32, jnp.bfloat16
    vm = pltpu.VMEM
    sem = lambda n: pltpu.SemaphoreType.DMA((n,))
    parts = lambda *lead: [vm(lead + (rows, 128), bf16) for rows in PARTS]
    held = {name: vm(a.shape, a.dtype) for name, a in zip(FETCHED, arrays)}
    return {
        **held,
        "fetch_sem": sem(len(FETCHED)),
        "leaving": vm((7, 256, 384), bf16),
        **{f"arrived{c}": vm((8, CHUNK, 384), bf16) for c in range(4)},
        "tile_send": sem(28), "tile_recv": sem(28),
        "cells": vm((3, 22 * WIDE * 8, 128), f32),
        "unit": vm((1024, 384), f32), "inv_std": vm((1024, 128), f32), "normed": vm((1024, 384), bf16),
        "hidden": vm((1024, 1536), bf16), "slope": vm((1024, 1536), bf16), "head_slope": vm((1024, 768), bf16),
        "depth": vm((ROWS_STEP, 384), f32), "section": vm((3, 1024, 128), f32), "embed_sum": vm((6, 8, 128), f32),
        "embed": vm((32, 128), bf16),
        "emb_all": vm((8, 32, 128), bf16), "rows_mine": vm((48, 128), bf16), "rows_all": vm((16, 48, 128), bf16),
        "wide": vm((34, 8, 128), f32), "grad_wide": vm((34, 8, 128), f32),
        "grad_mine": vm((48, 128), bf16), "grad_all": vm((8, 48, 128), bf16), "embed_grad": vm((48, 128), f32),
        "slide_send1": sem(7), "slide_recv1": sem(7), "slide_send2": sem(15), "slide_recv2": sem(15),
        "slide_send3": sem(7), "slide_recv3": sem(7),
        "grad_mlp": vm((1024, 384), bf16), "grad_pre": vm((1024, 1536), bf16), "depthwise": vm((1024, 384), f32),
        "flat": vm((4608, 128), f32), "flat2": vm((4616, 128), f32), "shares": vm((128, ROWS, 128), bf16),
        "taps": vm((168, 128), f32),
        "core_in": vm((4, 16, ROWS, 128), bf16),
        "s1": parts(4, 4, 4), "s2": parts(4, 4), "s3": parts(4),
        "r1": parts(3, 4, 4), "r2": parts(3, 4), "r3": parts(3),
        "core_send": sem(4), "core_recv": sem(4), "share_send": sem(27), "share_recv": sem(27),
        "share_sum": vm((ROWS, 128), f32),
        "tap_leaving": vm((7, 32, 128), bf16), "tap_arrived": vm((7, 32, 128), bf16), "tap_mine": vm((32, 128), bf16),
        "tap_group": vm((15, 32, 128), bf16), "tap_sum": vm((32, 128), f32), "tap_send": sem(22), "tap_recv": sem(22),
    }


def step_kernel(names, *refs):
    count = len(SCALARS) + len(FETCHED)
    ref = types.SimpleNamespace(**dict(zip(SCALARS, refs)))
    sources = refs[len(SCALARS):count]
    for name, one in zip(RESULTS, refs[count:]):
        setattr(ref, name, one)
    for name, one in zip(names, refs[count + len(RESULTS):]):
        setattr(ref, name, one)
    ref.fetches = [
        pltpu.make_async_copy(source, getattr(ref, name), ref.fetch_sem.at[i])
        for i, (name, source) in enumerate(zip(FETCHED, sources))
    ]
    for copy in ref.fetches:
        copy.start()
    dp, group = lax.axis_index("dp"), lax.axis_index("group")
    barrier = pltpu.get_barrier_semaphore()
    for k in range(1, 8):
        pl.semaphore_signal(barrier, inc=1, device_id=(lax.rem(dp + k, 8), group), device_id_type=MESH)
    for k in range(1, 16):
        pl.semaphore_signal(barrier, inc=1, device_id=(dp, lax.rem(group + k, 16)), device_id_type=MESH)
    departed = forward(ref, dp, group)
    copies = slide_pass(ref, dp, group)
    backward_weights(ref)
    shares = share_exchange(ref)
    next(shares)
    backward_norm(ref)
    next(shares)
    backward_depth(ref)
    taps = depth_exchange(ref, dp, group)
    next(taps)
    next(shares)
    next(taps)
    next(shares)
    for rest in (taps, shares):
        for _ in rest:
            pass
    for cp in copies:
        cp.wait_send()
    departed()


def training_step(*arrays):
    f32 = jnp.float32
    vm = pl.BlockSpec(memory_space=pltpu.VMEM)
    scratch = scratch_list(arrays[len(SCALARS):])
    out = jax.ShapeDtypeStruct
    return pl.pallas_call(
        functools.partial(step_kernel, tuple(scratch)),
        out_shape=(out((PROC, 256, 384), jnp.bfloat16), out((1, 768), f32), out((36, 128), f32), out((36, 128), f32),
                   out((8, 128), f32)),
        in_specs=[pl.BlockSpec(memory_space=pltpu.SMEM)] * len(SCALARS)
        + [pl.BlockSpec(memory_space=pl.ANY)] * len(FETCHED),
        out_specs=(vm,) * len(RESULTS),
        scratch_shapes=list(scratch.values()),
        compiler_params=pltpu.CompilerParams(collective_id=1, has_side_effects=True, vmem_limit_bytes=60 * 2**20),
        name="training_step",
    )(*arrays)


def on_device(
    tile_maps,
    positions,
    counts,
    routing,
    depth_kernel,
    depth_bias,
    norm_gain,
    norm_shift,
    expand_weight,
    expand_bias,
    reduce_weight,
    reduce_bias,
    layer_scale,
    head_weight,
    slide_taps,
    slide_weight,
    slide_bias,
    cotangent,
):
    tile_out, feature, expand_share, reduce_share, depth_share = training_step(
        counts,
        routing,
        positions,
        tile_maps.reshape(8, 256, 384),
        depth_kernel,
        depth_bias,
        norm_gain,
        norm_shift,
        expand_weight,
        expand_bias,
        reduce_weight,
        reduce_bias,
        layer_scale,
        head_weight,
        slide_taps,
        slide_weight,
        slide_bias,
        cotangent,
    )
    return (
        tile_out.reshape((PROC,) + tile_maps.shape[1:]),
        feature,
        expand_share.reshape(-1),
        reduce_share.reshape(-1),
        depth_share[:2].reshape(-1)[:147],
    )


def solution(mesh):
    return jax.shard_map(
        on_device,
        mesh=mesh,
        in_specs=(
            P(("dp", "group"), None, None, None),
            P(None, ("dp", "group")),
            P("dp"),
            P(None, "group", None),
            P(),
            P(),
            P(),
            P(),
            P(),
            P(),
            P(),
            P(),
            P(),
            P(),
            P(),
            P(),
            P(),
            P("dp", None),
        ),
        out_specs=(
            P(("dp", "group"), None, None, None),
            P("dp", None),
            P(("dp", "group")),
            P(("dp", "group")),
            P(("dp", "group")),
        ),
        check_vma=False,
    )
```

```python
import functools
import math
import types

import jax
import jax.numpy as jnp
from jax import lax
from jax.experimental import pallas as pl
from jax.experimental.pallas import tpu as pltpu
from jax.sharding import PartitionSpec as P

PROC = 4
EPSILON = 1e-06
HALF_ROOT = 0.7071067811865476
INV_ROOT_TAU = 0.3989422804014327
MESH = pl.DeviceIdType.MESH

WIDE = 14
STEP_U = 4
ROWS_STEP = STEP_U * 64
CHUNKS = (7, 4, 4, 1)
CHUNK_AT = (0, 7, 11, 15)


def nt_dot(left, right):
    return lax.dot_general(left, right, (((1,), (1,)), ((), ())), preferred_element_type=jnp.float32)


def tn_dot(left, right):
    return lax.dot_general(left, right, (((0,), (0,)), ((), ())), preferred_element_type=jnp.float32)


def gelu_and_slope(pre):
    phi = 0.5 + 0.5 * lax.erf(pre * HALF_ROOT)
    return pre * phi, phi + pre * (INV_ROOT_TAU * jnp.exp(-0.5 * (pre * pre)))


def tile_sources(routing, dp):
    source = []
    for q in range(PROC):
        found = -1
        for d in range(8):
            for s in range(8):
                found = jnp.where(routing[d, 0, s] == dp * PROC + q, d, found)
        source.append(found)
    return source


def emit_tiles(ref, source):
    def tile_row(u, carry):
        for q in range(PROC):
            for block in range(3):
                left = ref.section[block, pl.ds(u * 64 + q * 2, 8, stride=8), :]
                right = ref.section[block, pl.ds(u * 64 + q * 2 + 1, 8, stride=8), :]
                row = jnp.where(source[q] >= 0, jnp.concatenate([left, right], axis=0), 0.0)
                ref.tile_out[q, pl.ds(pl.multiple_of(u * 16, 16), 16), pl.ds(block * 128, 128)] = row.astype(jnp.bfloat16)
        return carry

    lax.fori_loop(0, 16, tile_row, 0)


def forward(ref, dp, group):
    f32, bf16 = jnp.float32, jnp.bfloat16
    routing, tiles, leaving, send, recv = ref.routing, ref.tiles, ref.leaving, ref.tile_send, ref.tile_recv
    cells, section, embed_sum, depth = ref.cells, ref.section, ref.embed_sum, ref.depth
    peers = [lax.rem(dp + k, 8) for k in range(8)]

    def slot_for(to):
        found = 0
        for s in range(1, 8):
            local = routing[dp, 0, s] - to * PROC
            found = jnp.where((local >= 0) & (local < PROC), s, found)
        return found

    slots = [slot_for(to) for to in peers]
    source = tile_sources(routing, dp)

    arrived = (ref.arrived0, ref.arrived1, ref.arrived2, ref.arrived3)

    def chunk_copy(c, k):
        return pltpu.make_async_remote_copy(
            src_ref=leaving.at[k - 1, pl.ds(CHUNK_AT[c] * 16, CHUNKS[c] * 16)], dst_ref=arrived[c].at[dp], send_sem=send.at[c * 7 + k - 1],
            recv_sem=recv.at[c * 7 + k - 1], device_id=(peers[k], group), device_id_type=MESH)

    pl.semaphore_wait(pltpu.get_barrier_semaphore(), 22)
    ref.fetches[0].wait()

    for c in range(4):
        rows = pl.ds(CHUNK_AT[c] * 16, CHUNKS[c] * 16)
        for k in (4, 5, 3, 2, 6, 1, 7):
            leaving[k - 1, rows, :] = tiles[slots[k], rows, :]
            chunk_copy(c, k).start()
        arrived[c][dp] = tiles[slots[0], rows, :]
    edge = 3 * WIDE * 8
    cells[:, 0:edge] = jnp.zeros((3, edge, 128), f32)
    cells[:, edge + 16 * WIDE * 8:] = jnp.zeros((3, edge, 128), f32)
    zeros3 = jnp.zeros((3, 128), f32)

    def fill(c, i):
        u = CHUNK_AT[c] + i
        base = (u + 3) * (WIDE * 8)
        for q in range(PROC):
            src = source[q]
            row = arrived[c][jnp.maximum(src, 0), i * 16:i * 16 + 16, :].astype(f32)
            row = jnp.where(src >= 0, row, 0.0)
            for block in range(3):
                lanes = slice(block * 128, block * 128 + 128)
                cells[block, pl.ds(base + q * 2, 3, stride=8), :] = zeros3
                cells[block, pl.ds(base + 24 + q * 2, 11, stride=8), :] = row[0:11, lanes]
                cells[block, pl.ds(base + q * 2 + 1, 11, stride=8), :] = row[5:16, lanes]
                cells[block, pl.ds(base + 88 + q * 2 + 1, 3, stride=8), :] = zeros3

    def land(c):
        for k in range(1, 8):
            chunk_copy(c, k).wait_recv()
        for i in range(CHUNKS[c]):
            fill(c, i)

    for copy in ref.fetches[1:]:
        copy.wait()
    land(0)
    embed_sum[...] = jnp.zeros((6, 8, 128), f32)

    def step(n, carry):
        start = pl.multiple_of(n * ROWS_STEP, ROWS_STEP)

        for c in range(1, 4):
            @pl.when(n == c)
            def _():
                land(c)

        for block in range(3):
            lanes = pl.ds(block * 128, 128)
            for part in range(STEP_U // 2):
                acc = [jnp.zeros((8, 8, 128), f32) + ref.depth_bias[lanes].reshape(1, 1, 128) for _ in range(2)]
                for a in range(8):
                    first = pl.multiple_of((n * STEP_U + part * 2 + a) * (WIDE * 8), 8)
                    x = cells[block, pl.ds(first, WIDE * 8), :].reshape(WIDE, 8, 128)
                    for i in range(2):
                        if 0 <= a - i < 7:
                            for b in range(7):
                                acc[i] = acc[i] + ref.depth_kernel[pl.ds((a - i) * 7 + b, 1), lanes].reshape(1, 1, 128) * x[b:b + 8]
                for i in range(2):
                    depth[pl.ds((part * 2 + i) * 64, 64), lanes] = acc[i].reshape(64, 128)
        value = depth[...]
        centred = value - jnp.mean(value, axis=1, keepdims=True)
        inv = lax.rsqrt(jnp.mean(centred * centred, axis=1, keepdims=True) + EPSILON)
        z = centred * inv
        ref.unit[pl.ds(start, ROWS_STEP), :] = z
        ref.inv_std[pl.ds(start, ROWS_STEP), :] = jnp.broadcast_to(inv, (ROWS_STEP, 128))
        norm = (z * ref.gain[...].reshape(1, 384) + ref.shift[...].reshape(1, 384)).astype(bf16)
        ref.normed[pl.ds(start, ROWS_STEP), :] = norm
        for m in range(6):
            cols = pl.ds(m * 256, 256)
            pre = jnp.dot(norm, ref.expand[:, cols], preferred_element_type=f32) + ref.expand_bias[cols].reshape(1, 256)
            act, grad = gelu_and_slope(pre)
            ref.hidden[pl.ds(start, ROWS_STEP), cols] = act.astype(bf16)
            ref.slope[pl.ds(start, ROWS_STEP), cols] = grad.astype(bf16)
        mlp = jnp.dot(ref.hidden[pl.ds(start, ROWS_STEP), :], ref.reduce[...], preferred_element_type=f32) + ref.reduce_bias[...].reshape(1, 384)
        mlp = mlp * ref.scale[...].reshape(1, 384)
        for i in range(STEP_U):
            first = pl.multiple_of((n * STEP_U + i + 3) * (WIDE * 8) + 24, 8)
            for block in range(3):
                section[block, pl.ds(pl.multiple_of(start + i * 64, 64), 64), :] = cells[block, pl.ds(first, 64), :] + mlp[i * 64:(i + 1) * 64, block * 128:block * 128 + 128]
        sec = jnp.concatenate([section[block, pl.ds(start, ROWS_STEP), :] for block in range(3)], axis=1).astype(bf16)
        for m in range(3):
            cols = pl.ds(m * 256, 256)
            act, grad = gelu_and_slope(jnp.dot(sec, ref.head[:, cols], preferred_element_type=f32))
            ref.head_slope[pl.ds(start, ROWS_STEP), cols] = grad.astype(bf16)
            act = jnp.sum(act.reshape(STEP_U * 8, 8, 256), axis=0)
            for half in range(2):
                embed_sum[m * 2 + half] = embed_sum[m * 2 + half] + act[:, half * 128:half * 128 + 128]
        return carry

    lax.fori_loop(0, 16 // STEP_U, step, 0)
    means = [
        (embed_sum[block, pl.ds(0, 4, stride=2), :] + embed_sum[block, pl.ds(1, 4, stride=2), :]) * (1.0 / 256.0)
        for block in range(6)
    ]
    ref.embed[...] = jnp.concatenate(means + [jnp.zeros((8, 128), f32)], axis=0).astype(bf16)

    def departed():
        for c in range(4):
            for k in range(1, 8):
                chunk_copy(c, k).wait_send()

    return departed


def slide_pass(ref, dp, group):
    routing, emb_all, rows_mine, rows_all = ref.routing, ref.emb_all, ref.rows_mine, ref.rows_all
    wide, grad_wide, grad_mine, grad_all = ref.wide, ref.grad_wide, ref.grad_mine, ref.grad_all
    f32, bf16, i32 = jnp.float32, jnp.bfloat16, jnp.int32
    dp_peers = [lax.rem(dp + k, 8) for k in range(1, 8)]
    group_peers = [lax.rem(group + k, 16) for k in range(1, 16)]

    def over_dp(source, landing, send, recv):
        copies = []
        for k, to in enumerate(dp_peers):
            cp = pltpu.make_async_remote_copy(src_ref=source, dst_ref=landing.at[dp], send_sem=send.at[k], recv_sem=recv.at[k], device_id=(to, group), device_id_type=MESH)
            cp.start()
            copies.append(cp)
        landing[dp] = source[...]
        return copies

    def iota(shape, axis):
        return lax.broadcasted_iota(i32, shape, axis)

    copies1 = over_dp(ref.embed, emb_all, ref.slide_send1, ref.slide_recv1)
    places = ref.count[0]

    row = iota((48, 128), 0)
    slot, block = row & 7, row >> 3
    channel = jnp.where(block >= 3, block - 3, block) * 128 + iota((48, 128), 1)
    spot = jnp.zeros((48, 128), i32)
    for s in range(8):
        spot = jnp.where(slot == s, jnp.where(block >= 3, ref.positions[1, s], ref.positions[0, s]), spot)
    frequency = jnp.exp((channel - (channel & 1)).astype(f32) * (-math.log(10000.0) / 384))
    angle = spot.astype(f32) * frequency
    pos_code = jnp.where((channel & 1) == 0, jnp.sin(angle), jnp.cos(angle))
    here = slot * 16 + group < places

    pick_row, pick_col = iota((48, 32), 0), iota((48, 32), 1)
    goes_to = jnp.full((48, 32), -1, i32)
    for s in range(8):
        goes_to = jnp.where((pick_row & 7) == s, routing[dp, 0, s], goes_to)
    goes_to = jnp.where((pick_row >> 3) == (pick_col >> 2), goes_to, -1)
    grad_row, grad_col = iota((48, 48), 0), iota((48, 48), 1)
    grad_place = jnp.where((grad_row >> 3) == (grad_col >> 3), dp * PROC + ((grad_row & 7) >> 1), -2)
    grad_picks = []
    for d in range(8):
        routed = jnp.full((48, 48), -1, i32)
        for s in range(8):
            routed = jnp.where((grad_col & 7) == s, routing[d, 0, s], routed)
        grad_picks.append(jnp.where(routed == grad_place, 1.0, 0.0).astype(bf16))

    emit_tiles(ref, tile_sources(routing, dp))
    for cp in copies1:
        cp.wait_recv()
    own = pos_code
    for e in range(8):
        pick = jnp.where(goes_to == e * PROC + (pick_col & 3), 1.0, 0.0).astype(bf16)
        own = own + jnp.dot(pick, emb_all[e], preferred_element_type=f32)
    rows_mine[...] = jnp.where(here, own, 0.0).astype(bf16)
    copies2 = []
    for k, to in enumerate(group_peers):
        cp = pltpu.make_async_remote_copy(src_ref=rows_mine, dst_ref=rows_all.at[group], send_sem=ref.slide_send2.at[k], recv_sem=ref.slide_recv2.at[k], device_id=(dp, to), device_id_type=MESH)
        cp.start()
        copies2.append(cp)
    rows_all[group] = rows_mine[...]
    for cp in copies2:
        cp.wait_recv()

    first, last = slot[0:8] == 0, slot[0:8] == 7

    def widen(block_rows, target):
        target[9:25] = block_rows
        for g in range(9):
            target[g] = jnp.where(first, 0.0, pltpu.roll(block_rows[g + 7], 1, 0))
            target[25 + g] = jnp.where(last, 0.0, pltpu.roll(block_rows[g], 7, 0))

    mixed = []
    for b in range(6):
        rows = rows_all[:, b * 8:b * 8 + 8, :].astype(f32)
        widen(rows, wide)
        total = rows
        for k in range(7):
            total = total + ref.slide_taps[pl.ds(k, 1), pl.ds(b * 128, 128)].reshape(1, 1, 128) * wide[3 * k:3 * k + 16]
        mixed.append(total.reshape(128, 128).astype(bf16))
    mixed = jnp.concatenate(mixed, axis=1)
    pre = jnp.dot(mixed, ref.slide_weight[...], preferred_element_type=f32) + ref.slide_bias[...].reshape(1, 768)
    seq_row = iota((128, 768), 0)
    share = jnp.where((seq_row & 7) * 16 + (seq_row >> 3) < places, 1.0, 0.0) / places.astype(f32)
    phi = 0.5 * (1.0 + lax.erf(pre * HALF_ROOT))
    slope = phi + pre * INV_ROOT_TAU * jnp.exp(-0.5 * pre * pre)
    grad_agg = (ref.cot[...] * share * slope).astype(bf16)
    grad_mixed = lax.dot_general(grad_agg, ref.slide_weight[...], (((1,), (1,)), ((), ())), preferred_element_type=f32)
    grad_rows = []
    for b in range(6):
        widen(grad_mixed[:, b * 128:b * 128 + 128].reshape(16, 8, 128), grad_wide)
        total = grad_wide[9 + group]
        for k in range(7):
            total = total + ref.slide_taps[pl.ds(k, 1), pl.ds(b * 128, 128)] * grad_wide[group + 18 - 3 * k]
        grad_rows.append(total)
    grad_mine[...] = jnp.where(here, jnp.concatenate(grad_rows, axis=0), 0.0).astype(bf16)
    copies3 = over_dp(grad_mine, grad_all, ref.slide_send3, ref.slide_recv3)
    ref.feature[...] = jnp.sum(pre * phi * share, axis=0, keepdims=True)
    for cp in copies3:
        cp.wait_recv()
    total = jnp.zeros((48, 128), f32)
    for d in range(8):
        total = total + jnp.dot(grad_picks[d], grad_all[d], preferred_element_type=f32)
    ref.embed_grad[...] = total
    return copies1 + copies2 + copies3


def backward_weights(ref):
    f32, bf16 = jnp.float32, jnp.bfloat16
    eg_row = jnp.concatenate([ref.embed_grad[8 * block:8 * block + 8] for block in range(6)], axis=1) * (1.0 / 256.0)

    def first(n, carry):
        rows = pl.ds(pl.multiple_of(n * 256, 256), 256)
        gh = (eg_row[None] * ref.head_slope[rows, :].astype(f32).reshape(32, 8, 768)).reshape(256, 768).astype(bf16)
        ref.grad_mlp[rows, :] = (ref.scale[...].reshape(1, 384) * nt_dot(gh, ref.head[...])).astype(bf16)
        return carry

    lax.fori_loop(0, 4, first, 0)

    for m in range(6):
        cols = pl.ds(m * 256, 256)
        for n in range(4):
            rows = pl.ds(n * 256, 256)
            gp = nt_dot(ref.grad_mlp[rows, :], ref.reduce[cols, :]) * ref.slope[rows, cols].astype(f32)
            ref.grad_pre[rows, cols] = gp.astype(bf16)
        eg_m = tn_dot(ref.normed[...], ref.grad_pre[:, cols])
        for l in range(2):
            ref.flat[pl.ds(m * 2 + l, 384, stride=12), :] = eg_m[:, l * 128:(l + 1) * 128]
    for m in range(6):
        rg_m = tn_dot(ref.hidden[:, pl.ds(m * 256, 256)], ref.grad_mlp[...])
        for l in range(3):
            ref.flat2[pl.ds(m * 768 + l, 256, stride=3), :] = rg_m[:, l * 128:(l + 1) * 128]

    ref.flat2[4608:] = jnp.zeros((8, 128), f32)

    def pack(i, carry):
        ref.shares[i, 0:32] = ref.flat[pl.ds(i * 36, 32), :].astype(bf16)
        ref.shares[i, 32:48] = jnp.concatenate(
            [ref.flat[pl.ds(i * 36 + 32, 4), :], jnp.zeros((4, 128), f32), ref.flat2[pl.ds(i * 36, 8), :]], axis=0
        ).astype(bf16)
        ref.shares[i, 48:80] = ref.flat2[pl.ds(i * 36 + 8, 32), :].astype(bf16)
        return carry

    lax.fori_loop(0, 128, pack, 0)


def backward_norm(ref):
    f32, bf16 = jnp.float32, jnp.bfloat16

    def second(n, carry):
        rows = pl.ds(pl.multiple_of(n * 256, 256), 256)
        w = nt_dot(ref.grad_pre[rows, :], ref.expand[...]) * ref.gain[...].reshape(1, 384)
        z = ref.unit[rows, :]
        inv = jnp.concatenate([ref.inv_std[rows, :]] * 3, axis=1)
        ref.depthwise[rows, :] = inv * (w - jnp.mean(w, axis=1, keepdims=True) - z * jnp.mean(w * z, axis=1, keepdims=True))
        return carry

    lax.fori_loop(0, 4, second, 0)


def backward_depth(ref):
    f32 = jnp.float32
    ref.taps[147:] = jnp.zeros((21, 128), f32)
    for block in range(3):
        lanes = pl.ds(block * 128, 128)
        for a in range(7):
            def row(u, acc):
                g = ref.depthwise[pl.ds(pl.multiple_of(u * 64, 64), 64), lanes].reshape(8, 8, 128)
                x = ref.cells[block, pl.ds(pl.multiple_of((u + a) * (WIDE * 8), 8), WIDE * 8), :].reshape(WIDE, 8, 128)
                return tuple(acc[b] + jnp.sum(g * x[b:b + 8], axis=0) for b in range(7))
            acc = lax.fori_loop(0, 16, row, tuple(jnp.zeros((8, 128), f32) for _ in range(7)))
            for b in range(7):
                ref.taps[pl.ds((a * 7 + b) * 3 + block, 1), :] = jnp.sum(acc[b], axis=0, keepdims=True)


def depth_exchange(ref, dp, group):
    f32, bf16 = jnp.float32, jnp.bfloat16
    copies = []
    for k in range(1, 8):
        to = lax.rem(dp + k, 8)
        ref.tap_leaving[k - 1] = ref.taps[pl.ds(lax.div(147 * to, 8), 32), :].astype(bf16)
        cp = pltpu.make_async_remote_copy(src_ref=ref.tap_leaving.at[k - 1], dst_ref=ref.tap_arrived.at[k - 1], send_sem=ref.tap_send.at[k - 1], recv_sem=ref.tap_recv.at[k - 1], device_id=(to, group), device_id_type=MESH)
        cp.start()
        copies.append(cp)
    yield
    total = ref.taps[pl.ds(lax.div(147 * dp, 8), 32), :]
    for cp in copies:
        cp.wait_recv()
    for k in range(7):
        total = total + ref.tap_arrived[k].astype(f32)
    ref.tap_mine[...] = total.astype(bf16)
    for k in range(1, 16):
        to = lax.rem(group + k, 16)
        cp = pltpu.make_async_remote_copy(src_ref=ref.tap_mine, dst_ref=ref.tap_group.at[k - 1], send_sem=ref.tap_send.at[6 + k], recv_sem=ref.tap_recv.at[6 + k], device_id=(dp, to), device_id_type=MESH)
        cp.start()
        copies.append(cp)
    yield
    for cp in copies[7:]:
        cp.wait_recv()
    for k in range(15):
        total = total + ref.tap_group[k].astype(f32)
    ref.tap_sum[...] = total
    begin = 147 * (16 * dp + group)
    row = lax.div(begin, 128) - lax.div(147 * dp, 8)
    turn = lax.rem(begin, 128)
    near = pltpu.roll(ref.tap_sum[pl.ds(row, 8), :], 128 - turn, 1)
    lane = lax.broadcasted_iota(jnp.int32, (8, 128), 1)
    ref.depth_out[...] = jnp.where(lane < 128 - turn, near, pltpu.roll(near, 7, 0))
    for cp in copies:
        cp.wait_send()


PARTS = (32, 32, 16)
ORDERS = ("yxz", "xzy", "zyx")
ROWS = sum(PARTS)

def torus_place():
    dp, group = lax.axis_index("dp"), lax.axis_index("group")
    return {"y": lax.div(dp, 2), "c": lax.rem(dp, 2), "x": lax.div(group, 4), "z": lax.rem(group, 4)}

def torus_device(place, **moved):
    at = {**place, **moved}
    return (at["y"] * 2 + at["c"], at["x"] * 4 + at["z"])

def share_exchange(ref):
    place = torus_place()
    partner = torus_device(place, c=1 - place["c"])
    core_in, core_send, core_recv, send, recv = ref.core_in, ref.core_send, ref.core_recv, ref.share_send, ref.share_recv
    s1, s2, s3, r1, r2, r3 = ref.s1, ref.s2, ref.s3, ref.r1, ref.r2, ref.r3
    core_copies = []
    for y in range(4):
        cp = pltpu.make_async_remote_copy(src_ref=ref.shares.at[pl.ds(pl.multiple_of((y * 2 + 1 - place["c"]) * 16, 16), 16)], dst_ref=core_in.at[y], send_sem=core_send.at[y], recv_sem=core_recv.at[y], device_id=partner, device_id_type=MESH)
        cp.start()
        core_copies.append(cp)

    def start(stage, part, source, landing):
        axis = ORDERS[part][stage]
        made = []
        for k in (2, 1, 3):
            to = lax.rem(place[axis] + k, 4)
            cp = pltpu.make_async_remote_copy(src_ref=source.at[to], dst_ref=landing.at[k - 1], send_sem=send.at[stage * 9 + part * 3 + k - 1], recv_sem=recv.at[stage * 9 + part * 3 + k - 1], device_id=torus_device(place, **{axis: to}), device_id_type=MESH)
            cp.start()
            made.append(cp)
        return made

    yield
    f32 = jnp.float32
    for y in range(4):
        core_copies[y].wait_recv()
        for x in range(4):
            both = ref.shares[pl.ds((y * 2 + place["c"]) * 16 + x * 4, 4)].astype(f32) + core_in[y, x * 4:x * 4 + 4].astype(f32)
            both = both.astype(jnp.bfloat16)
            s1[0][y, x] = both[:, 0:32]
            s1[1][x, :, y] = both[:, 32:64]
            for z in range(4):
                s1[2][z, y, x] = both[z, 64:80]
    flying = [start(0, part, s1[part], r1[part]) for part in range(3)]
    yield
    flying2 = []
    for part in range(3):
        for cp in flying[part]:
            cp.wait_recv()
        mine = place[ORDERS[part][0]]
        for a in range(4):
            total = s1[part][mine, a].astype(f32)
            for k in range(3):
                total = total + r1[part][k, a].astype(f32)
            s2[part][a] = total.astype(jnp.bfloat16)
        flying2.append(start(1, part, s2[part], r2[part]))
    yield
    flying3 = []
    for part in range(3):
        for cp in flying2[part]:
            cp.wait_recv()
        mine = place[ORDERS[part][1]]
        total = s2[part][mine].astype(f32)
        for k in range(3):
            total = total + r2[part][k].astype(f32)
        s3[part][...] = total.astype(jnp.bfloat16)
        flying3.append(start(2, part, s3[part], r3[part]))
    yield
    base = 0
    for part in range(3):
        for cp in flying3[part]:
            cp.wait_recv()
        total = s3[part][place[ORDERS[part][2]]].astype(f32)
        for k in range(3):
            total = total + r3[part][k].astype(f32)
        ref.share_sum[base:base + PARTS[part]] = total
        base += PARTS[part]
    ref.expand_out[...] = ref.share_sum[0:36]
    ref.reduce_out[...] = ref.share_sum[40:76]
    for cp in core_copies:
        cp.wait_send()
    for copies in flying + flying2 + flying3:
        for cp in copies:
            cp.wait_send()


SCALARS = ("count", "routing", "positions")
FETCHED = ("tiles", "depth_kernel", "depth_bias", "gain", "shift", "expand", "expand_bias", "reduce", "reduce_bias",
           "scale", "head", "slide_taps", "slide_weight", "slide_bias", "cot")
RESULTS = ("tile_out", "feature", "expand_out", "reduce_out", "depth_out")


def scratch_list(arrays):
    f32, bf16 = jnp.float32, jnp.bfloat16
    vm = pltpu.VMEM
    sem = lambda n: pltpu.SemaphoreType.DMA((n,))
    parts = lambda *lead: [vm(lead + (rows, 128), bf16) for rows in PARTS]
    held = {name: vm(a.shape, a.dtype) for name, a in zip(FETCHED, arrays)}
    return {
        **held,
        "fetch_sem": sem(len(FETCHED)),
        "leaving": vm((7, 256, 384), bf16),
        **{f"arrived{c}": vm((8, rows * 16, 384), bf16) for c, rows in enumerate(CHUNKS)},
        "tile_send": sem(28), "tile_recv": sem(28),
        "cells": vm((3, 22 * WIDE * 8, 128), f32),
        "unit": vm((1024, 384), f32), "inv_std": vm((1024, 128), f32), "normed": vm((1024, 384), bf16),
        "hidden": vm((1024, 1536), bf16), "slope": vm((1024, 1536), bf16), "head_slope": vm((1024, 768), bf16),
        "depth": vm((ROWS_STEP, 384), f32), "section": vm((3, 1024, 128), f32), "embed_sum": vm((6, 8, 128), f32),
        "embed": vm((32, 128), bf16),
        "emb_all": vm((8, 32, 128), bf16), "rows_mine": vm((48, 128), bf16), "rows_all": vm((16, 48, 128), bf16),
        "wide": vm((34, 8, 128), f32), "grad_wide": vm((34, 8, 128), f32),
        "grad_mine": vm((48, 128), bf16), "grad_all": vm((8, 48, 128), bf16), "embed_grad": vm((48, 128), f32),
        "slide_send1": sem(7), "slide_recv1": sem(7), "slide_send2": sem(15), "slide_recv2": sem(15),
        "slide_send3": sem(7), "slide_recv3": sem(7),
        "grad_mlp": vm((1024, 384), bf16), "grad_pre": vm((1024, 1536), bf16), "depthwise": vm((1024, 384), f32),
        "flat": vm((4608, 128), f32), "flat2": vm((4616, 128), f32), "shares": vm((128, ROWS, 128), bf16),
        "taps": vm((168, 128), f32),
        "core_in": vm((4, 16, ROWS, 128), bf16),
        "s1": parts(4, 4, 4), "s2": parts(4, 4), "s3": parts(4),
        "r1": parts(3, 4, 4), "r2": parts(3, 4), "r3": parts(3),
        "core_send": sem(4), "core_recv": sem(4), "share_send": sem(27), "share_recv": sem(27),
        "share_sum": vm((ROWS, 128), f32),
        "tap_leaving": vm((7, 32, 128), bf16), "tap_arrived": vm((7, 32, 128), bf16), "tap_mine": vm((32, 128), bf16),
        "tap_group": vm((15, 32, 128), bf16), "tap_sum": vm((32, 128), f32), "tap_send": sem(22), "tap_recv": sem(22),
    }


def step_kernel(names, *refs):
    count = len(SCALARS) + len(FETCHED)
    ref = types.SimpleNamespace(**dict(zip(SCALARS, refs)))
    sources = refs[len(SCALARS):count]
    for name, one in zip(RESULTS, refs[count:]):
        setattr(ref, name, one)
    for name, one in zip(names, refs[count + len(RESULTS):]):
        setattr(ref, name, one)
    ref.fetches = [
        pltpu.make_async_copy(source, getattr(ref, name), ref.fetch_sem.at[i])
        for i, (name, source) in enumerate(zip(FETCHED, sources))
    ]
    for copy in ref.fetches:
        copy.start()
    dp, group = lax.axis_index("dp"), lax.axis_index("group")
    barrier = pltpu.get_barrier_semaphore()
    for k in range(1, 8):
        pl.semaphore_signal(barrier, inc=1, device_id=(lax.rem(dp + k, 8), group), device_id_type=MESH)
    for k in range(1, 16):
        pl.semaphore_signal(barrier, inc=1, device_id=(dp, lax.rem(group + k, 16)), device_id_type=MESH)
    departed = forward(ref, dp, group)
    copies = slide_pass(ref, dp, group)
    backward_weights(ref)
    shares = share_exchange(ref)
    next(shares)
    backward_norm(ref)
    next(shares)
    backward_depth(ref)
    taps = depth_exchange(ref, dp, group)
    next(taps)
    next(shares)
    next(taps)
    next(shares)
    for rest in (taps, shares):
        for _ in rest:
            pass
    for cp in copies:
        cp.wait_send()
    departed()


def training_step(*arrays):
    f32 = jnp.float32
    vm = pl.BlockSpec(memory_space=pltpu.VMEM)
    scratch = scratch_list(arrays[len(SCALARS):])
    out = jax.ShapeDtypeStruct
    return pl.pallas_call(
        functools.partial(step_kernel, tuple(scratch)),
        out_shape=(out((PROC, 256, 384), jnp.bfloat16), out((1, 768), f32), out((36, 128), f32), out((36, 128), f32),
                   out((8, 128), f32)),
        in_specs=[pl.BlockSpec(memory_space=pltpu.SMEM)] * len(SCALARS)
        + [pl.BlockSpec(memory_space=pl.ANY)] * len(FETCHED),
        out_specs=(vm,) * len(RESULTS),
        scratch_shapes=list(scratch.values()),
        compiler_params=pltpu.CompilerParams(collective_id=1, has_side_effects=True, vmem_limit_bytes=60 * 2**20),
        name="training_step",
    )(*arrays)


def finish_kernel(*refs):
    for i in range(4):
        refs[5 + i][...] = refs[i][...]
    refs[9][0:128] = refs[4][0]
    refs[9][128:147] = refs[4][1, 0:19]


def finish(*arrays):
    vm = pl.BlockSpec(memory_space=pltpu.VMEM)
    return pl.pallas_call(
        finish_kernel,
        out_shape=tuple(jax.ShapeDtypeStruct(a.shape, a.dtype) for a in arrays[:4]) + (jax.ShapeDtypeStruct((147,), jnp.float32),),
        in_specs=[vm] * 5,
        out_specs=(vm,) * 5,
        name="finish",
    )(*arrays)


def on_device(
    tile_maps,
    positions,
    counts,
    routing,
    depth_kernel,
    depth_bias,
    norm_gain,
    norm_shift,
    expand_weight,
    expand_bias,
    reduce_weight,
    reduce_bias,
    layer_scale,
    head_weight,
    slide_taps,
    slide_weight,
    slide_bias,
    cotangent,
):
    results = training_step(
        counts,
        routing,
        positions,
        tile_maps.reshape(8, 256, 384),
        depth_kernel,
        depth_bias,
        norm_gain,
        norm_shift,
        expand_weight,
        expand_bias,
        reduce_weight,
        reduce_bias,
        layer_scale,
        head_weight,
        slide_taps,
        slide_weight,
        slide_bias,
        cotangent,
    )
    tile_out, feature, expand_share, reduce_share, depth_share = finish(*results)
    return (
        tile_out.reshape((PROC,) + tile_maps.shape[1:]),
        feature,
        expand_share.reshape(-1),
        reduce_share.reshape(-1),
        depth_share,
    )


def solution(mesh):
    return jax.shard_map(
        on_device,
        mesh=mesh,
        in_specs=(
            P(("dp", "group"), None, None, None),
            P(None, ("dp", "group")),
            P("dp"),
            P(None, "group", None),
            P(),
            P(),
            P(),
            P(),
            P(),
            P(),
            P(),
            P(),
            P(),
            P(),
            P(),
            P(),
            P(),
            P("dp", None),
        ),
        out_specs=(
            P(("dp", "group"), None, None, None),
            P("dp", None),
            P(("dp", "group")),
            P(("dp", "group")),
            P(("dp", "group")),
        ),
        check_vma=False,
    )
```

```python
import functools
import math
import types

import jax
import jax.numpy as jnp
from jax import lax
from jax.experimental import pallas as pl
from jax.experimental.pallas import tpu as pltpu
from jax.sharding import PartitionSpec as P

PROC = 4
EPSILON = 1e-06
HALF_ROOT = 0.7071067811865476
INV_ROOT_TAU = 0.3989422804014327
MESH = pl.DeviceIdType.MESH

WIDE = 14
STEP_U = 4
ROWS_STEP = STEP_U * 64
CHUNKS = (7, 4, 4, 1)
CHUNK_AT = (0, 7, 11, 15)


def nt_dot(left, right):
    return lax.dot_general(left, right, (((1,), (1,)), ((), ())), preferred_element_type=jnp.float32)


def tn_dot(left, right):
    return lax.dot_general(left, right, (((0,), (0,)), ((), ())), preferred_element_type=jnp.float32)


def gelu_and_slope(pre):
    phi = 0.5 + 0.5 * lax.erf(pre * HALF_ROOT)
    return pre * phi, phi + pre * (INV_ROOT_TAU * jnp.exp(-0.5 * (pre * pre)))


def tile_sources(routing, dp):
    source = []
    for q in range(PROC):
        found = -1
        for d in range(8):
            for s in range(8):
                found = jnp.where(routing[d, 0, s] == dp * PROC + q, d, found)
        source.append(found)
    return source


def emit_tiles(ref, source):
    def tile_row(u, carry):
        for q in range(PROC):
            for block in range(3):
                left = ref.section[block, pl.ds(u * 64 + q * 2, 8, stride=8), :]
                right = ref.section[block, pl.ds(u * 64 + q * 2 + 1, 8, stride=8), :]
                row = jnp.where(source[q] >= 0, jnp.concatenate([left, right], axis=0), 0.0)
                ref.tile_out[q, pl.ds(pl.multiple_of(u * 16, 16), 16), pl.ds(block * 128, 128)] = row.astype(jnp.bfloat16)
        return carry

    lax.fori_loop(0, 16, tile_row, 0)


def forward(ref, dp, group):
    f32, bf16 = jnp.float32, jnp.bfloat16
    routing, tiles, leaving, send, recv = ref.routing, ref.tiles, ref.leaving, ref.tile_send, ref.tile_recv
    cells, section, embed_sum, depth = ref.cells, ref.section, ref.embed_sum, ref.depth
    peers = [lax.rem(dp + k, 8) for k in range(8)]

    def slot_for(to):
        found = 0
        for s in range(1, 8):
            local = routing[dp, 0, s] - to * PROC
            found = jnp.where((local >= 0) & (local < PROC), s, found)
        return found

    slots = [slot_for(to) for to in peers]
    source = tile_sources(routing, dp)

    arrived = (ref.arrived0, ref.arrived1, ref.arrived2, ref.arrived3)

    def chunk_copy(c, k):
        return pltpu.make_async_remote_copy(
            src_ref=leaving.at[k - 1, pl.ds(CHUNK_AT[c] * 16, CHUNKS[c] * 16)], dst_ref=arrived[c].at[dp], send_sem=send.at[c * 7 + k - 1],
            recv_sem=recv.at[c * 7 + k - 1], device_id=(peers[k], group), device_id_type=MESH)

    pl.semaphore_wait(pltpu.get_barrier_semaphore(), 22)
    ref.fetches[0].wait()

    for c in range(4):
        rows = pl.ds(CHUNK_AT[c] * 16, CHUNKS[c] * 16)
        for k in (4, 5, 3, 2, 6, 1, 7):
            leaving[k - 1, rows, :] = tiles[slots[k], rows, :]
            chunk_copy(c, k).start()
        arrived[c][dp] = tiles[slots[0], rows, :]
    edge = 3 * WIDE * 8
    cells[:, 0:edge] = jnp.zeros((3, edge, 128), f32)
    cells[:, edge + 16 * WIDE * 8:] = jnp.zeros((3, edge, 128), f32)
    zeros3 = jnp.zeros((3, 128), f32)

    def fill(c, i):
        u = CHUNK_AT[c] + i
        base = (u + 3) * (WIDE * 8)
        for q in range(PROC):
            src = source[q]
            row = arrived[c][jnp.maximum(src, 0), i * 16:i * 16 + 16, :].astype(f32)
            row = jnp.where(src >= 0, row, 0.0)
            for block in range(3):
                lanes = slice(block * 128, block * 128 + 128)
                cells[block, pl.ds(base + q * 2, 3, stride=8), :] = zeros3
                cells[block, pl.ds(base + 24 + q * 2, 11, stride=8), :] = row[0:11, lanes]
                cells[block, pl.ds(base + q * 2 + 1, 11, stride=8), :] = row[5:16, lanes]
                cells[block, pl.ds(base + 88 + q * 2 + 1, 3, stride=8), :] = zeros3

    def land(c):
        for k in range(1, 8):
            chunk_copy(c, k).wait_recv()
        for i in range(CHUNKS[c]):
            fill(c, i)

    for copy in ref.fetches[1:]:
        copy.wait()
    land(0)
    embed_sum[...] = jnp.zeros((6, 8, 128), f32)

    def step(n, carry):
        start = pl.multiple_of(n * ROWS_STEP, ROWS_STEP)

        for c in range(1, 4):
            @pl.when(n == c)
            def _():
                land(c)

        for block in range(3):
            lanes = pl.ds(block * 128, 128)
            for part in range(STEP_U // 2):
                acc = [jnp.zeros((8, 8, 128), f32) + ref.depth_bias[lanes].reshape(1, 1, 128) for _ in range(2)]
                for a in range(8):
                    first = pl.multiple_of((n * STEP_U + part * 2 + a) * (WIDE * 8), 8)
                    x = cells[block, pl.ds(first, WIDE * 8), :].reshape(WIDE, 8, 128)
                    for i in range(2):
                        if 0 <= a - i < 7:
                            for b in range(7):
                                acc[i] = acc[i] + ref.depth_kernel[pl.ds((a - i) * 7 + b, 1), lanes].reshape(1, 1, 128) * x[b:b + 8]
                for i in range(2):
                    depth[pl.ds((part * 2 + i) * 64, 64), lanes] = acc[i].reshape(64, 128)
        value = depth[...]
        centred = value - jnp.mean(value, axis=1, keepdims=True)
        inv = lax.rsqrt(jnp.mean(centred * centred, axis=1, keepdims=True) + EPSILON)
        z = centred * inv
        ref.unit[pl.ds(start, ROWS_STEP), :] = z
        ref.inv_std[pl.ds(start, ROWS_STEP), :] = jnp.broadcast_to(inv, (ROWS_STEP, 128))
        norm = (z * ref.gain[...].reshape(1, 384) + ref.shift[...].reshape(1, 384)).astype(bf16)
        ref.normed[pl.ds(start, ROWS_STEP), :] = norm
        for m in range(6):
            cols = pl.ds(m * 256, 256)
            pre = jnp.dot(norm, ref.expand[:, cols], preferred_element_type=f32) + ref.expand_bias[cols].reshape(1, 256)
            act, grad = gelu_and_slope(pre)
            ref.hidden[pl.ds(start, ROWS_STEP), cols] = act.astype(bf16)
            ref.slope[pl.ds(start, ROWS_STEP), cols] = grad.astype(bf16)
        mlp = jnp.dot(ref.hidden[pl.ds(start, ROWS_STEP), :], ref.reduce[...], preferred_element_type=f32) + ref.reduce_bias[...].reshape(1, 384)
        mlp = mlp * ref.scale[...].reshape(1, 384)
        for i in range(STEP_U):
            first = pl.multiple_of((n * STEP_U + i + 3) * (WIDE * 8) + 24, 8)
            for block in range(3):
                section[block, pl.ds(pl.multiple_of(start + i * 64, 64), 64), :] = cells[block, pl.ds(first, 64), :] + mlp[i * 64:(i + 1) * 64, block * 128:block * 128 + 128]
        sec = jnp.concatenate([section[block, pl.ds(start, ROWS_STEP), :] for block in range(3)], axis=1).astype(bf16)
        for m in range(3):
            cols = pl.ds(m * 256, 256)
            act, grad = gelu_and_slope(jnp.dot(sec, ref.head[:, cols], preferred_element_type=f32))
            ref.head_slope[pl.ds(start, ROWS_STEP), cols] = grad.astype(bf16)
            act = jnp.sum(act.reshape(STEP_U * 8, 8, 256), axis=0)
            for half in range(2):
                embed_sum[m * 2 + half] = embed_sum[m * 2 + half] + act[:, half * 128:half * 128 + 128]
        return carry

    lax.fori_loop(0, 16 // STEP_U, step, 0)
    means = [
        (embed_sum[block, pl.ds(0, 4, stride=2), :] + embed_sum[block, pl.ds(1, 4, stride=2), :]) * (1.0 / 256.0)
        for block in range(6)
    ]
    ref.embed[...] = jnp.concatenate(means + [jnp.zeros((8, 128), f32)], axis=0).astype(bf16)

    def departed():
        for c in range(4):
            for k in range(1, 8):
                chunk_copy(c, k).wait_send()

    return departed


def far_first(group):
    x, z = lax.div(group, 4), lax.rem(group, 4)
    moves = [(i, j) for i in range(4) for j in range(4) if i or j]
    moves.sort(key=lambda move: -sum(min(step, 4 - step) for step in move))
    return [lax.rem(x + i, 4) * 4 + lax.rem(z + j, 4) for i, j in moves]


def slide_pass(ref, dp, group):
    routing, emb_all, rows_mine, rows_all = ref.routing, ref.emb_all, ref.rows_mine, ref.rows_all
    wide, grad_wide, grad_mine, grad_all = ref.wide, ref.grad_wide, ref.grad_mine, ref.grad_all
    f32, bf16, i32 = jnp.float32, jnp.bfloat16, jnp.int32
    dp_peers = [lax.rem(dp + k, 8) for k in range(1, 8)]
    group_peers = far_first(group)

    def over_dp(source, landing, send, recv):
        copies = []
        for k, to in enumerate(dp_peers):
            cp = pltpu.make_async_remote_copy(src_ref=source, dst_ref=landing.at[dp], send_sem=send.at[k], recv_sem=recv.at[k], device_id=(to, group), device_id_type=MESH)
            cp.start()
            copies.append(cp)
        landing[dp] = source[...]
        return copies

    def iota(shape, axis):
        return lax.broadcasted_iota(i32, shape, axis)

    copies1 = over_dp(ref.embed, emb_all, ref.slide_send1, ref.slide_recv1)
    places = ref.count[0]

    row = iota((48, 128), 0)
    slot, block = row & 7, row >> 3
    channel = jnp.where(block >= 3, block - 3, block) * 128 + iota((48, 128), 1)
    spot = jnp.zeros((48, 128), i32)
    for s in range(8):
        spot = jnp.where(slot == s, jnp.where(block >= 3, ref.positions[1, s], ref.positions[0, s]), spot)
    frequency = jnp.exp((channel - (channel & 1)).astype(f32) * (-math.log(10000.0) / 384))
    angle = spot.astype(f32) * frequency
    pos_code = jnp.where((channel & 1) == 0, jnp.sin(angle), jnp.cos(angle))
    here = slot * 16 + group < places

    pick_row, pick_col = iota((48, 32), 0), iota((48, 32), 1)
    goes_to = jnp.full((48, 32), -1, i32)
    for s in range(8):
        goes_to = jnp.where((pick_row & 7) == s, routing[dp, 0, s], goes_to)
    goes_to = jnp.where((pick_row >> 3) == (pick_col >> 2), goes_to, -1)
    grad_row, grad_col = iota((48, 48), 0), iota((48, 48), 1)
    grad_place = jnp.where((grad_row >> 3) == (grad_col >> 3), dp * PROC + ((grad_row & 7) >> 1), -2)
    grad_picks = []
    for d in range(8):
        routed = jnp.full((48, 48), -1, i32)
        for s in range(8):
            routed = jnp.where((grad_col & 7) == s, routing[d, 0, s], routed)
        grad_picks.append(jnp.where(routed == grad_place, 1.0, 0.0).astype(bf16))

    emit_tiles(ref, tile_sources(routing, dp))
    for cp in copies1:
        cp.wait_recv()
    own = pos_code
    for e in range(8):
        pick = jnp.where(goes_to == e * PROC + (pick_col & 3), 1.0, 0.0).astype(bf16)
        own = own + jnp.dot(pick, emb_all[e], preferred_element_type=f32)
    rows_mine[...] = jnp.where(here, own, 0.0).astype(bf16)
    copies2 = []
    for k, to in enumerate(group_peers):
        cp = pltpu.make_async_remote_copy(src_ref=rows_mine, dst_ref=rows_all.at[group], send_sem=ref.slide_send2.at[k], recv_sem=ref.slide_recv2.at[k], device_id=(dp, to), device_id_type=MESH)
        cp.start()
        copies2.append(cp)
    rows_all[group] = rows_mine[...]
    for cp in copies2:
        cp.wait_recv()

    first, last = slot[0:8] == 0, slot[0:8] == 7

    def widen(block_rows, target):
        target[9:25] = block_rows
        for g in range(9):
            target[g] = jnp.where(first, 0.0, pltpu.roll(block_rows[g + 7], 1, 0))
            target[25 + g] = jnp.where(last, 0.0, pltpu.roll(block_rows[g], 7, 0))

    mixed = []
    for b in range(6):
        rows = rows_all[:, b * 8:b * 8 + 8, :].astype(f32)
        widen(rows, wide)
        total = rows
        for k in range(7):
            total = total + ref.slide_taps[pl.ds(k, 1), pl.ds(b * 128, 128)].reshape(1, 1, 128) * wide[3 * k:3 * k + 16]
        mixed.append(total.reshape(128, 128).astype(bf16))
    mixed = jnp.concatenate(mixed, axis=1)
    pre = jnp.dot(mixed, ref.slide_weight[...], preferred_element_type=f32) + ref.slide_bias[...].reshape(1, 768)
    seq_row = iota((128, 768), 0)
    share = jnp.where((seq_row & 7) * 16 + (seq_row >> 3) < places, 1.0, 0.0) / places.astype(f32)
    phi = 0.5 * (1.0 + lax.erf(pre * HALF_ROOT))
    slope = phi + pre * INV_ROOT_TAU * jnp.exp(-0.5 * pre * pre)
    grad_agg = (ref.cot[...] * share * slope).astype(bf16)
    grad_mixed = lax.dot_general(grad_agg, ref.slide_weight[...], (((1,), (1,)), ((), ())), preferred_element_type=f32)
    grad_rows = []
    for b in range(6):
        widen(grad_mixed[:, b * 128:b * 128 + 128].reshape(16, 8, 128), grad_wide)
        total = grad_wide[9 + group]
        for k in range(7):
            total = total + ref.slide_taps[pl.ds(k, 1), pl.ds(b * 128, 128)] * grad_wide[group + 18 - 3 * k]
        grad_rows.append(total)
    grad_mine[...] = jnp.where(here, jnp.concatenate(grad_rows, axis=0), 0.0).astype(bf16)
    copies3 = over_dp(grad_mine, grad_all, ref.slide_send3, ref.slide_recv3)
    ref.feature[...] = jnp.sum(pre * phi * share, axis=0, keepdims=True)
    for cp in copies3:
        cp.wait_recv()
    total = jnp.zeros((48, 128), f32)
    for d in range(8):
        total = total + jnp.dot(grad_picks[d], grad_all[d], preferred_element_type=f32)
    ref.embed_grad[...] = total
    return copies1 + copies2 + copies3


def backward_weights(ref):
    f32, bf16 = jnp.float32, jnp.bfloat16
    eg_row = jnp.concatenate([ref.embed_grad[8 * block:8 * block + 8] for block in range(6)], axis=1) * (1.0 / 256.0)

    def first(n, carry):
        rows = pl.ds(pl.multiple_of(n * 256, 256), 256)
        gh = (eg_row[None] * ref.head_slope[rows, :].astype(f32).reshape(32, 8, 768)).reshape(256, 768).astype(bf16)
        ref.grad_mlp[rows, :] = (ref.scale[...].reshape(1, 384) * nt_dot(gh, ref.head[...])).astype(bf16)
        return carry

    lax.fori_loop(0, 4, first, 0)

    for m in range(6):
        cols = pl.ds(m * 256, 256)
        for n in range(4):
            rows = pl.ds(n * 256, 256)
            gp = nt_dot(ref.grad_mlp[rows, :], ref.reduce[cols, :]) * ref.slope[rows, cols].astype(f32)
            ref.grad_pre[rows, cols] = gp.astype(bf16)
        eg_m = tn_dot(ref.normed[...], ref.grad_pre[:, cols])
        for l in range(2):
            ref.flat[pl.ds(m * 2 + l, 384, stride=12), :] = eg_m[:, l * 128:(l + 1) * 128]
    for m in range(6):
        rg_m = tn_dot(ref.hidden[:, pl.ds(m * 256, 256)], ref.grad_mlp[...])
        for l in range(3):
            ref.flat2[pl.ds(m * 768 + l, 256, stride=3), :] = rg_m[:, l * 128:(l + 1) * 128]

    ref.flat2[4608:] = jnp.zeros((8, 128), f32)

    def pack(i, carry):
        ref.shares[i, 0:32] = ref.flat[pl.ds(i * 36, 32), :].astype(bf16)
        ref.shares[i, 32:48] = jnp.concatenate(
            [ref.flat[pl.ds(i * 36 + 32, 4), :], jnp.zeros((4, 128), f32), ref.flat2[pl.ds(i * 36, 8), :]], axis=0
        ).astype(bf16)
        ref.shares[i, 48:80] = ref.flat2[pl.ds(i * 36 + 8, 32), :].astype(bf16)
        return carry

    lax.fori_loop(0, 128, pack, 0)


def backward_norm(ref):
    f32, bf16 = jnp.float32, jnp.bfloat16

    def second(n, carry):
        rows = pl.ds(pl.multiple_of(n * 256, 256), 256)
        w = nt_dot(ref.grad_pre[rows, :], ref.expand[...]) * ref.gain[...].reshape(1, 384)
        z = ref.unit[rows, :]
        inv = jnp.concatenate([ref.inv_std[rows, :]] * 3, axis=1)
        ref.depthwise[rows, :] = inv * (w - jnp.mean(w, axis=1, keepdims=True) - z * jnp.mean(w * z, axis=1, keepdims=True))
        return carry

    lax.fori_loop(0, 4, second, 0)


def backward_depth(ref):
    f32 = jnp.float32
    ref.taps[147:] = jnp.zeros((21, 128), f32)
    for block in range(3):
        lanes = pl.ds(block * 128, 128)
        for a in range(7):
            def row(u, acc):
                g = ref.depthwise[pl.ds(pl.multiple_of(u * 64, 64), 64), lanes].reshape(8, 8, 128)
                x = ref.cells[block, pl.ds(pl.multiple_of((u + a) * (WIDE * 8), 8), WIDE * 8), :].reshape(WIDE, 8, 128)
                return tuple(acc[b] + jnp.sum(g * x[b:b + 8], axis=0) for b in range(7))
            acc = lax.fori_loop(0, 16, row, tuple(jnp.zeros((8, 128), f32) for _ in range(7)))
            for b in range(7):
                ref.taps[pl.ds((a * 7 + b) * 3 + block, 1), :] = jnp.sum(acc[b], axis=0, keepdims=True)


def depth_exchange(ref, dp, group):
    f32, bf16 = jnp.float32, jnp.bfloat16
    copies = []
    for k in range(1, 8):
        to = lax.rem(dp + k, 8)
        ref.tap_leaving[k - 1] = ref.taps[pl.ds(lax.div(147 * to, 8), 32), :].astype(bf16)
        cp = pltpu.make_async_remote_copy(src_ref=ref.tap_leaving.at[k - 1], dst_ref=ref.tap_arrived.at[k - 1], send_sem=ref.tap_send.at[k - 1], recv_sem=ref.tap_recv.at[k - 1], device_id=(to, group), device_id_type=MESH)
        cp.start()
        copies.append(cp)
    yield
    total = ref.taps[pl.ds(lax.div(147 * dp, 8), 32), :]
    for cp in copies:
        cp.wait_recv()
    for k in range(7):
        total = total + ref.tap_arrived[k].astype(f32)
    ref.tap_mine[...] = total.astype(bf16)
    for k, to in enumerate(far_first(group), 1):
        cp = pltpu.make_async_remote_copy(src_ref=ref.tap_mine, dst_ref=ref.tap_group.at[k - 1], send_sem=ref.tap_send.at[6 + k], recv_sem=ref.tap_recv.at[6 + k], device_id=(dp, to), device_id_type=MESH)
        cp.start()
        copies.append(cp)
    yield
    for cp in copies[7:]:
        cp.wait_recv()
    for k in range(15):
        total = total + ref.tap_group[k].astype(f32)
    ref.tap_sum[...] = total
    begin = 147 * (16 * dp + group)
    row = lax.div(begin, 128) - lax.div(147 * dp, 8)
    turn = lax.rem(begin, 128)
    near = pltpu.roll(ref.tap_sum[pl.ds(row, 8), :], 128 - turn, 1)
    lane = lax.broadcasted_iota(jnp.int32, (8, 128), 1)
    ref.depth_out[...] = jnp.where(lane < 128 - turn, near, pltpu.roll(near, 7, 0))
    for cp in copies:
        cp.wait_send()


PARTS = (32, 32, 16)
ORDERS = ("yxz", "xzy", "zyx")
ROWS = sum(PARTS)

def torus_place():
    dp, group = lax.axis_index("dp"), lax.axis_index("group")
    return {"y": lax.div(dp, 2), "c": lax.rem(dp, 2), "x": lax.div(group, 4), "z": lax.rem(group, 4)}

def torus_device(place, **moved):
    at = {**place, **moved}
    return (at["y"] * 2 + at["c"], at["x"] * 4 + at["z"])

def share_exchange(ref):
    place = torus_place()
    partner = torus_device(place, c=1 - place["c"])
    core_in, core_send, core_recv, send, recv = ref.core_in, ref.core_send, ref.core_recv, ref.share_send, ref.share_recv
    s1, s2, s3, r1, r2, r3 = ref.s1, ref.s2, ref.s3, ref.r1, ref.r2, ref.r3
    core_copies = []
    for y in range(4):
        cp = pltpu.make_async_remote_copy(src_ref=ref.shares.at[pl.ds(pl.multiple_of((y * 2 + 1 - place["c"]) * 16, 16), 16)], dst_ref=core_in.at[y], send_sem=core_send.at[y], recv_sem=core_recv.at[y], device_id=partner, device_id_type=MESH)
        cp.start()
        core_copies.append(cp)

    def start(stage, part, source, landing):
        axis = ORDERS[part][stage]
        made = []
        for k in (2, 1, 3):
            to = lax.rem(place[axis] + k, 4)
            cp = pltpu.make_async_remote_copy(src_ref=source.at[to], dst_ref=landing.at[k - 1], send_sem=send.at[stage * 9 + part * 3 + k - 1], recv_sem=recv.at[stage * 9 + part * 3 + k - 1], device_id=torus_device(place, **{axis: to}), device_id_type=MESH)
            cp.start()
            made.append(cp)
        return made

    yield
    f32 = jnp.float32
    for y in range(4):
        core_copies[y].wait_recv()
        for x in range(4):
            both = ref.shares[pl.ds((y * 2 + place["c"]) * 16 + x * 4, 4)].astype(f32) + core_in[y, x * 4:x * 4 + 4].astype(f32)
            both = both.astype(jnp.bfloat16)
            s1[0][y, x] = both[:, 0:32]
            s1[1][x, :, y] = both[:, 32:64]
            for z in range(4):
                s1[2][z, y, x] = both[z, 64:80]
    flying = [start(0, part, s1[part], r1[part]) for part in range(3)]
    yield
    flying2 = []
    for part in range(3):
        for cp in flying[part]:
            cp.wait_recv()
        mine = place[ORDERS[part][0]]
        for a in range(4):
            total = s1[part][mine, a].astype(f32)
            for k in range(3):
                total = total + r1[part][k, a].astype(f32)
            s2[part][a] = total.astype(jnp.bfloat16)
        flying2.append(start(1, part, s2[part], r2[part]))
    yield
    flying3 = []
    for part in range(3):
        for cp in flying2[part]:
            cp.wait_recv()
        mine = place[ORDERS[part][1]]
        total = s2[part][mine].astype(f32)
        for k in range(3):
            total = total + r2[part][k].astype(f32)
        s3[part][...] = total.astype(jnp.bfloat16)
        flying3.append(start(2, part, s3[part], r3[part]))
    yield
    base = 0
    for part in range(3):
        for cp in flying3[part]:
            cp.wait_recv()
        total = s3[part][place[ORDERS[part][2]]].astype(f32)
        for k in range(3):
            total = total + r3[part][k].astype(f32)
        ref.share_sum[base:base + PARTS[part]] = total
        base += PARTS[part]
    ref.expand_out[...] = ref.share_sum[0:36]
    ref.reduce_out[...] = ref.share_sum[40:76]
    for cp in core_copies:
        cp.wait_send()
    for copies in flying + flying2 + flying3:
        for cp in copies:
            cp.wait_send()


SCALARS = ("count", "routing", "positions")
FETCHED = ("tiles", "depth_kernel", "depth_bias", "gain", "shift", "expand", "expand_bias", "reduce", "reduce_bias",
           "scale", "head", "slide_taps", "slide_weight", "slide_bias", "cot")
RESULTS = ("tile_out", "feature", "expand_out", "reduce_out", "depth_out")


def scratch_list(arrays):
    f32, bf16 = jnp.float32, jnp.bfloat16
    vm = pltpu.VMEM
    sem = lambda n: pltpu.SemaphoreType.DMA((n,))
    parts = lambda *lead: [vm(lead + (rows, 128), bf16) for rows in PARTS]
    held = {name: vm(a.shape, a.dtype) for name, a in zip(FETCHED, arrays)}
    return {
        **held,
        "fetch_sem": sem(len(FETCHED)),
        "leaving": vm((7, 256, 384), bf16),
        **{f"arrived{c}": vm((8, rows * 16, 384), bf16) for c, rows in enumerate(CHUNKS)},
        "tile_send": sem(28), "tile_recv": sem(28),
        "cells": vm((3, 22 * WIDE * 8, 128), f32),
        "unit": vm((1024, 384), f32), "inv_std": vm((1024, 128), f32), "normed": vm((1024, 384), bf16),
        "hidden": vm((1024, 1536), bf16), "slope": vm((1024, 1536), bf16), "head_slope": vm((1024, 768), bf16),
        "depth": vm((ROWS_STEP, 384), f32), "section": vm((3, 1024, 128), f32), "embed_sum": vm((6, 8, 128), f32),
        "embed": vm((32, 128), bf16),
        "emb_all": vm((8, 32, 128), bf16), "rows_mine": vm((48, 128), bf16), "rows_all": vm((16, 48, 128), bf16),
        "wide": vm((34, 8, 128), f32), "grad_wide": vm((34, 8, 128), f32),
        "grad_mine": vm((48, 128), bf16), "grad_all": vm((8, 48, 128), bf16), "embed_grad": vm((48, 128), f32),
        "slide_send1": sem(7), "slide_recv1": sem(7), "slide_send2": sem(15), "slide_recv2": sem(15),
        "slide_send3": sem(7), "slide_recv3": sem(7),
        "grad_mlp": vm((1024, 384), bf16), "grad_pre": vm((1024, 1536), bf16), "depthwise": vm((1024, 384), f32),
        "flat": vm((4608, 128), f32), "flat2": vm((4616, 128), f32), "shares": vm((128, ROWS, 128), bf16),
        "taps": vm((168, 128), f32),
        "core_in": vm((4, 16, ROWS, 128), bf16),
        "s1": parts(4, 4, 4), "s2": parts(4, 4), "s3": parts(4),
        "r1": parts(3, 4, 4), "r2": parts(3, 4), "r3": parts(3),
        "core_send": sem(4), "core_recv": sem(4), "share_send": sem(27), "share_recv": sem(27),
        "share_sum": vm((ROWS, 128), f32),
        "tap_leaving": vm((7, 32, 128), bf16), "tap_arrived": vm((7, 32, 128), bf16), "tap_mine": vm((32, 128), bf16),
        "tap_group": vm((15, 32, 128), bf16), "tap_sum": vm((32, 128), f32), "tap_send": sem(22), "tap_recv": sem(22),
    }


def step_kernel(names, *refs):
    count = len(SCALARS) + len(FETCHED)
    ref = types.SimpleNamespace(**dict(zip(SCALARS, refs)))
    sources = refs[len(SCALARS):count]
    for name, one in zip(RESULTS, refs[count:]):
        setattr(ref, name, one)
    for name, one in zip(names, refs[count + len(RESULTS):]):
        setattr(ref, name, one)
    ref.fetches = [
        pltpu.make_async_copy(source, getattr(ref, name), ref.fetch_sem.at[i])
        for i, (name, source) in enumerate(zip(FETCHED, sources))
    ]
    for copy in ref.fetches:
        copy.start()
    dp, group = lax.axis_index("dp"), lax.axis_index("group")
    barrier = pltpu.get_barrier_semaphore()
    for k in range(1, 8):
        pl.semaphore_signal(barrier, inc=1, device_id=(lax.rem(dp + k, 8), group), device_id_type=MESH)
    for k in range(1, 16):
        pl.semaphore_signal(barrier, inc=1, device_id=(dp, lax.rem(group + k, 16)), device_id_type=MESH)
    departed = forward(ref, dp, group)
    copies = slide_pass(ref, dp, group)
    backward_weights(ref)
    shares = share_exchange(ref)
    next(shares)
    backward_norm(ref)
    next(shares)
    backward_depth(ref)
    taps = depth_exchange(ref, dp, group)
    next(taps)
    next(shares)
    next(taps)
    next(shares)
    for rest in (taps, shares):
        for _ in rest:
            pass
    for cp in copies:
        cp.wait_send()
    departed()


def training_step(*arrays):
    f32 = jnp.float32
    vm = pl.BlockSpec(memory_space=pltpu.VMEM)
    scratch = scratch_list(arrays[len(SCALARS):])
    out = jax.ShapeDtypeStruct
    return pl.pallas_call(
        functools.partial(step_kernel, tuple(scratch)),
        out_shape=(out((PROC, 256, 384), jnp.bfloat16), out((1, 768), f32), out((36, 128), f32), out((36, 128), f32),
                   out((8, 128), f32)),
        in_specs=[pl.BlockSpec(memory_space=pltpu.SMEM)] * len(SCALARS)
        + [pl.BlockSpec(memory_space=pl.ANY)] * len(FETCHED),
        out_specs=(vm,) * len(RESULTS),
        scratch_shapes=list(scratch.values()),
        compiler_params=pltpu.CompilerParams(collective_id=1, has_side_effects=True, vmem_limit_bytes=60 * 2**20),
        name="training_step",
    )(*arrays)


def finish_kernel(*refs):
    for i in range(4):
        refs[5 + i][...] = refs[i][...]
    refs[9][0:128] = refs[4][0]
    refs[9][128:147] = refs[4][1, 0:19]


def finish(*arrays):
    vm = pl.BlockSpec(memory_space=pltpu.VMEM)
    return pl.pallas_call(
        finish_kernel,
        out_shape=tuple(jax.ShapeDtypeStruct(a.shape, a.dtype) for a in arrays[:4]) + (jax.ShapeDtypeStruct((147,), jnp.float32),),
        in_specs=[vm] * 5,
        out_specs=(vm,) * 5,
        name="finish",
    )(*arrays)


def on_device(
    tile_maps,
    positions,
    counts,
    routing,
    depth_kernel,
    depth_bias,
    norm_gain,
    norm_shift,
    expand_weight,
    expand_bias,
    reduce_weight,
    reduce_bias,
    layer_scale,
    head_weight,
    slide_taps,
    slide_weight,
    slide_bias,
    cotangent,
):
    results = training_step(
        counts,
        routing,
        positions,
        tile_maps.reshape(8, 256, 384),
        depth_kernel,
        depth_bias,
        norm_gain,
        norm_shift,
        expand_weight,
        expand_bias,
        reduce_weight,
        reduce_bias,
        layer_scale,
        head_weight,
        slide_taps,
        slide_weight,
        slide_bias,
        cotangent,
    )
    tile_out, feature, expand_share, reduce_share, depth_share = finish(*results)
    return (
        tile_out.reshape((PROC,) + tile_maps.shape[1:]),
        feature,
        expand_share.reshape(-1),
        reduce_share.reshape(-1),
        depth_share,
    )


def solution(mesh):
    return jax.shard_map(
        on_device,
        mesh=mesh,
        in_specs=(
            P(("dp", "group"), None, None, None),
            P(None, ("dp", "group")),
            P("dp"),
            P(None, "group", None),
            P(),
            P(),
            P(),
            P(),
            P(),
            P(),
            P(),
            P(),
            P(),
            P(),
            P(),
            P(),
            P(),
            P("dp", None),
        ),
        out_specs=(
            P(("dp", "group"), None, None, None),
            P("dp", None),
            P(("dp", "group")),
            P(("dp", "group")),
            P(("dp", "group")),
        ),
        check_vma=False,
    )
```
